256 devices in a mesh: dom: 16 (over x_hi, y, core), shard: 8 (over z), dp: 2 (over x_lo).
Axes of the slice: x: 4 (x_hi: 2, x_lo: 2; x = x_hi * 2 + x_lo), y: 4, z: 8, core: 2. Of those that a mesh axis runs over, the one named last changes fastest.
Arguments:
- queries_in: bfloat16 [16, 2048, 1024], P('dom', ('shard', 'dp')), may hold values from -8 to 8
- encoder_weight: bfloat16 [1024, 1024], P(('dom', 'shard', 'dp')), may hold values from -0.1875 to 0.1875
- codebook: float32 [16, 128, 8, 256], P('dom', 'shard'), may hold values from -0.06 to 0.06
- codes: int32 [16, 8192, 128], P('dom', 'shard'), may hold values from 0 to 255
- positive_ids: int32 [16, 2048], P('dom'), may hold values from 0 to 8191
- loss_weight: bfloat16 [16, 2048], P('dom'), may hold values from 0.5 to 2
Outputs:
- encoder_grad: float32 [1024, 1024], P(('dom', 'shard', 'dp'))
- codebook_grad: float32 [16, 128, 8, 256], P('dom', ('shard', 'dp'))
The draws below stay inside these ranges and needn't reach their ends.
All inputs are finite; a program needn't handle non-finite values.
Results may differ from the reference program's by a relative error of at most 0.0005.
The reference program's roundings to bfloat16 on the way (of `normed_low`, `book`, `passages`, `grad_scores` and `grad_encoded`) count: a program that leaves them out, or rounds other values in their place, can miss the bound.
Values may be sent and summed in bfloat16 or wider, within the bound.
A program may use at most 64 MiB of HBM per device.

```python
import math
import jax
import jax.numpy as jnp
from jax import lax

D = 1024
M = 128
K = 256
SUB = 8
PARTS_SIZE = 16
QUERIES = 2048
PASSAGES = 8192


def draw_queries_in(key, part):
    keys = jax.random.split(key, 4)
    base = jax.random.normal(keys[0], (PARTS_SIZE, QUERIES, D), jnp.float32)
    rows = jnp.exp(jax.random.uniform(keys[1], (PARTS_SIZE, QUERIES, 1), jnp.float32, math.log(0.3), math.log(3.0)))
    cols = jnp.exp(jax.random.uniform(keys[3], (D,), jnp.float32, math.log(0.5), math.log(2.0)))
    values = base * rows * cols
    return jnp.clip(values, -8.0, 8.0).astype(jnp.bfloat16)


def place_ends(result, key, low, largest):
    shape = result.shape
    place = [jax.random.randint(jax.random.fold_in(key, axis), (), 0, shape[axis]) for axis in range(len(shape))]
    result = result.at[tuple(place)].set(low)
    longest = shape.index(max(shape))
    place[longest] = (place[longest] + 1) % shape[longest]
    return result.at[tuple(place)].set(largest)


def block_levels(own_key, shape, cuts, smallest, largest):
    gain, own = 1.0, jax.random.fold_in(own_key, 6)
    for position, shards_of in cuts:
        heights = jnp.exp(jax.random.uniform(jax.random.fold_in(own, position), (shards_of,), jnp.float32, smallest / len(cuts), largest / len(cuts)))
        gain = gain * jnp.repeat(heights, shape[position] // shards_of).reshape([-1 if axis == position else 1 for axis in range(len(shape))])
    return gain


def bell_draw(key, dims, deviation, bound, shards=(), held_as=jnp.bfloat16):
    drawn = jax.random.normal(key, dims, jnp.float32) * deviation
    if len(shards) > 0:
        drawn = block_levels(key, dims, shards, -0.22, 0.18) * drawn
    return jnp.clip(drawn, min=-bound, max=bound).astype(held_as)


def setup_inputs(seed: int = 0) -> dict:
    streams_of = jax.random.split(jax.random.key(seed), 7)
    queries_in = draw_queries_in(jax.random.fold_in(streams_of[6], 71), 0)
    encoder_weight = bell_draw(streams_of[1], (D, D), D ** -0.5, 0.1875, ((0, 256),))
    codebook = jnp.clip(jax.random.uniform(streams_of[2], (PARTS_SIZE, M, SUB, K), jnp.float32, -0.06, 0.06) * block_levels(streams_of[2], (PARTS_SIZE, M, SUB, K), ((0, 16), (1, 8)), -0.4, 0.0), -0.06, 0.06)
    codes = place_ends(jax.random.randint(streams_of[3], (PARTS_SIZE, PASSAGES, M), 0, K), jax.random.fold_in(streams_of[3], 1), 0, K - 1).astype(jnp.int32)
    positive_ids = place_ends(jax.random.randint(streams_of[4], (PARTS_SIZE, QUERIES), 0, PASSAGES), jax.random.fold_in(streams_of[4], 1), 0, PASSAGES - 1).astype(jnp.int32)
    loss_weight = jnp.clip(jnp.exp(math.log(2.0) - 1.3862944 * jax.random.uniform(streams_of[5], (PARTS_SIZE, QUERIES), jnp.float32) ** block_levels(streams_of[5], (PARTS_SIZE, QUERIES), ((0, 16),), -0.2, 0.2)), 0.5, 2.0).astype(jnp.bfloat16)
    return dict(queries_in=queries_in, encoder_weight=encoder_weight, codebook=codebook, codes=codes, positive_ids=positive_ids, loss_weight=loss_weight)


def rebuild(codes_part, book):
    levels = jnp.arange(K, dtype=jnp.int32)

    def one_sub(pair):
        column, words = pair
        onehot = (column[:, None] == levels[None, :]).astype(jnp.bfloat16)
        return lax.dot_general(onehot, words, (((1,), (1,)), ((), ())), preferred_element_type=jnp.float32)
    pieces = lax.map(one_sub, (codes_part.T, book))
    return jnp.transpose(pieces, (1, 0, 2)).reshape(codes_part.shape[0], -1).astype(jnp.bfloat16)

def word_grads(codes_part, grad_passages):
    levels = jnp.arange(K, dtype=jnp.int32)
    split = jnp.transpose(grad_passages.reshape(codes_part.shape[0], M, SUB), (1, 0, 2))

    def one_sub(pair):
        column, grads = pair
        onehot = (column[:, None] == levels[None, :]).astype(jnp.float32)
        return lax.dot_general(grads, onehot, (((0,), (0,)), ((), ())), precision=lax.Precision.HIGHEST, preferred_element_type=jnp.float32)
    return lax.map(one_sub, (codes_part.T, split))

def reference(queries_in, encoder_weight, codebook, codes, positive_ids, loss_weight):

    def partition(items):
        inputs, master, codes_part, positive, weights = items
        encoded = jnp.dot(inputs, encoder_weight, preferred_element_type=jnp.float32)
        inv_rms = lax.rsqrt(lax.optimization_barrier(jnp.mean(encoded * encoded, axis=1, keepdims=True)) + 1e-06)
        normed = encoded * inv_rms
        normed_low = normed.astype(jnp.bfloat16)
        passages = rebuild(codes_part, master.astype(jnp.bfloat16))
        scores = lax.dot_general(normed_low, passages, (((1,), (1,)), ((), ())), preferred_element_type=jnp.float32)
        exps = jnp.exp(scores)
        prob = exps / lax.optimization_barrier(jnp.sum(exps, axis=1, keepdims=True))
        target = (positive[:, None] == jnp.arange(PASSAGES, dtype=jnp.int32)[None, :]).astype(jnp.float32)
        grad_scores = (weights.astype(jnp.float32)[:, None] * (prob - target)).astype(jnp.bfloat16)
        grad_normed = jnp.dot(grad_scores, passages, preferred_element_type=jnp.float32)
        grad_passages = lax.dot_general(grad_scores, normed_low, (((0,), (0,)), ((), ())), preferred_element_type=jnp.float32)
        book_grad = word_grads(codes_part, grad_passages)
        inner = lax.optimization_barrier(jnp.mean(grad_normed * normed, axis=1, keepdims=True))
        grad_encoded = (inv_rms * (grad_normed - normed * inner)).astype(jnp.bfloat16)
        weight_grad = lax.dot_general(inputs, grad_encoded, (((0,), (0,)), ((), ())), preferred_element_type=jnp.float32)
        return (weight_grad, book_grad)
    weight_grads, book_grads = lax.map(partition, (queries_in, codebook, codes, positive_ids, loss_weight))
    return (lax.optimization_barrier(jnp.sum(weight_grads, axis=0)), book_grads)
```

```python
import functools

import jax
import jax.numpy as jnp
from jax import lax
from jax.experimental import pallas as pl
from jax.experimental.pallas import tpu as pltpu
from jax.sharding import PartitionSpec as P

MESH = pl.DeviceIdType.MESH
BF16 = jnp.bfloat16
F32 = jnp.float32
EPS = 1e-06
NT = (((1,), (1,)), ((), ()))


class Ring:
    def __init__(self, slot, half, me, n, dev, send_sem, recv_sem):
        self.slot, self.half, self.me, self.n, self.dev = slot, half, me, n, dev
        self.send_sem, self.recv_sem, self.k = send_sem, recv_sem, n // 2

    def at(self, offset):
        return lax.rem(self.me + offset + self.n, self.n)

    def copies(self, s, shift):
        views = (self.slot, self.slot) if s < self.k - 1 else (lambda i: self.half(i, 0), lambda i: self.half(i, 1))
        out = []
        for way, sign in ((0, 1), (1, -1)):
            ref = views[way](self.at(-sign * (s + shift)))
            out.append(
                pltpu.make_async_remote_copy(
                    src_ref=ref,
                    dst_ref=ref,
                    send_sem=self.send_sem.at[way, s],
                    recv_sem=self.recv_sem.at[way, s],
                    device_id=self.dev(self.at(sign)),
                    device_id_type=MESH,
                )
            )
        return out

    def start(self, s):
        for copy in self.copies(s, 0):
            copy.start()

    def recv(self, s):
        for copy in self.copies(s, 1):
            copy.wait_recv()

    def finish(self):
        for s in range(self.k):
            for copy in self.copies(s, 0):
                copy.wait_send()


def kernel(
    sizes,
    w_ref,
    x_ref,
    book_ref,
    codes_ref,
    pos_ref,
    wt_ref,
    wg_ref,
    cg_ref,
    g_all,
    w_full,
    xt,
    books,
    codes_t,
    pt,
    pas,
    qs,
    q_cat,
    exps,
    gs_cat,
    gn,
    slots,
    gpt,
    normed_t,
    tots,
    a1_s,
    a1_r,
    a2_s,
    a2_r,
    y_s,
    y_r,
    core_s,
    core_r,
    book_s,
    book_r,
    q_s,
    q_r,
    tot_s,
    tot_r,
    gn_s,
    gn_r,
):
    xh_n, y_n, c_n, z_n, x_n = sizes
    dom, z, x = lax.axis_index("dom"), lax.axis_index("shard"), lax.axis_index("dp")
    xh, y, c = dom // (y_n * c_n), lax.rem(dom // c_n, y_n), lax.rem(dom, c_n)

    def dom_of(xh_, y_, c_):
        return (xh_ * y_n + y_) * c_n + c_

    def dev(dom_=None, z_=None, x_=None):
        return {
            "dom": dom if dom_ is None else dom_,
            "shard": z if z_ is None else z_,
            "dp": x if x_ is None else x_,
        }

    def turn(i, d, n):
        return lax.rem(i + d + n, n)

    in_group = [(dz, dx) for dz in range(z_n) for dx in range(x_n) if (dz, dx) != (0, 0)]
    peers = [dev(z_=turn(z, dz, z_n), x_=turn(x, dx, x_n)) for dz, dx in in_group]
    peers += [dev(dom_of(turn(xh, 1, xh_n), y, c))]
    peers += [dev(dom_of(xh, turn(y, dy, y_n), c)) for dy in range(1, y_n)]
    peers += [dev(dom_of(xh, y, turn(c, 1, c_n)))]
    barrier = pltpu.get_barrier_semaphore()
    for peer in peers:
        pl.semaphore_signal(barrier, inc=1, device_id=peer, device_id_type=MESH)

    mine = z * x_n + x
    g_all[dom, mine] = w_ref[...]
    books[z] = book_ref[...].astype(BF16)
    pl.semaphore_wait(barrier, len(peers))

    def a1(i, back):
        dz, dx = in_group[i]
        sign = -1 if back else 1
        z_, x_ = turn(z, sign * dz, z_n), turn(x, sign * dx, x_n)
        ref = g_all.at[dom, z_ * x_n + x_ if back else mine]
        return pltpu.make_async_remote_copy(
            src_ref=ref,
            dst_ref=ref,
            send_sem=a1_s.at[i],
            recv_sem=a1_r.at[i],
            device_id=dev(z_=z_, x_=x_),
            device_id_type=MESH,
        )

    for i in range(len(in_group)):
        a1(i, False).start()
    book_ring = Ring(
        lambda i: books.at[i],
        lambda i, h: books.at[i, pl.ds(h * (books.shape[1] // 2), books.shape[1] // 2)],
        z,
        z_n,
        lambda i: dev(z_=i),
        book_s,
        book_r,
    )
    book_ring.start(0)

    n_sub, n_pass = codes_t.shape
    for i in range(n_pass // 128):
        codes_t[:, i * 128 : (i + 1) * 128] = codes_ref[i * 128 : (i + 1) * 128, :].T
    for i in range(x_ref.shape[1] // 128):
        xt[i * 128 : (i + 1) * 128, :] = x_ref[:, i * 128 : (i + 1) * 128].astype(F32).T.astype(BF16)

    for i in range(len(in_group)):
        a1(i, True).wait_recv()

    xh2 = turn(xh, 1, xh_n)

    def a2(back):
        ref = g_all.at[dom_of(xh2 if back else xh, y, c)]
        return pltpu.make_async_remote_copy(
            src_ref=ref,
            dst_ref=ref,
            send_sem=a2_s,
            recv_sem=a2_r,
            device_id=dev(dom_of(xh2, y, c)),
            device_id_type=MESH,
        )

    def y_ring(j, xh_):
        half = g_all.shape[1] // 2
        return Ring(
            lambda i: g_all.at[dom_of(xh_, i, c)],
            lambda i, h: g_all.at[dom_of(xh_, i, c), pl.ds(h * half, half)],
            y,
            y_n,
            lambda i: dev(dom_of(xh, i, c)),
            y_s.at[j],
            y_r.at[j],
        )

    def core(j, dy, back):
        ref = g_all.at[dom_of(xh2 if j else xh, turn(y, dy, y_n), turn(c, 1, c_n) if back else c)]
        return pltpu.make_async_remote_copy(
            src_ref=ref,
            dst_ref=ref,
            send_sem=core_s.at[j, dy],
            recv_sem=core_r.at[j, dy],
            device_id=dev(dom_of(xh, y, turn(c, 1, c_n))),
            device_id_type=MESH,
        )

    blk, col_blocks = w_ref.shape[0], x_ref.shape[1] // 128
    r_rows = blk // col_blocks
    per = 16 // r_rows
    rows = blk * per
    o = lax.broadcasted_iota(jnp.int32, (rows, rows), 0)
    j_ = lax.broadcasted_iota(jnp.int32, (rows, rows), 1)
    perm = (
        (j_ == (lax.rem(o, 16) // r_rows) * blk + (o // 16) * r_rows + lax.rem(o, r_rows)).astype(F32).astype(BF16)
    )

    def assemble(dom_):
        for t in range(g_all.shape[1] // per):
            part = jnp.dot(
                perm, g_all[dom_, t * per : (t + 1) * per].reshape(rows, 128), preferred_element_type=F32
            ).astype(BF16)
            row = pl.multiple_of((dom_ * (g_all.shape[1] // per) + t) * 16, 16)
            for cb in range(col_blocks):
                w_full[pl.ds(row, 16), cb * 128 : (cb + 1) * 128] = part[cb * 16 : (cb + 1) * 16]

    def rebuild(zb):
        groups = books.shape[1] // 64

        def per_group(gi, carry):
            r = pl.multiple_of(gi * 64, 64)
            table = books[zb, pl.ds(r, 64), :].astype(F32)
            out_row = pl.multiple_of(zb * books.shape[1] + r, 64)
            code_row = pl.multiple_of((zb * groups + gi) * 8, 8)

            def per_block(i, inner):
                for u in range(2):
                    p0 = pl.multiple_of(i * 256 + u * 128, 128)
                    cc = codes_t[pl.ds(code_row, 8), pl.ds(p0, 128)]
                    for jj in range(4):
                        parts = []
                        for j in (2 * jj, 2 * jj + 1):
                            idx = jnp.broadcast_to(cc[j : j + 1, :], (8, 128))
                            low = idx & 127
                            lo = jnp.take_along_axis(
                                table[j * 8 : j * 8 + 8, :128], low, axis=1, mode="promise_in_bounds"
                            )
                            hi = jnp.take_along_axis(
                                table[j * 8 : j * 8 + 8, 128:], low, axis=1, mode="promise_in_bounds"
                            )
                            parts.append(jnp.where(idx >= 128, hi, lo))
                        pt[pl.ds(pl.multiple_of(out_row + jj * 16, 16), 16), pl.ds(p0, 128)] = jnp.concatenate(
                            parts, 0
                        ).astype(BF16)
                return inner

            return lax.fori_loop(0, n_pass // 256, per_block, carry)

        lax.fori_loop(0, groups, per_group, 0)

    ring0, ring1 = y_ring(0, xh), y_ring(1, xh2)
    a2(False).start()
    ring0.start(0)
    core(0, 0, False).start()
    rebuild(z)
    book_ring.recv(0)
    book_ring.start(1)
    a2(True).wait_recv()
    ring1.start(0)
    core(1, 0, False).start()
    rebuild(turn(z, 1, z_n))
    ring0.recv(0)
    ring0.start(1)
    core(0, 1, False).start()
    core(0, 3, False).start()
    rebuild(turn(z, -1, z_n))
    book_ring.recv(1)
    book_ring.start(2)
    ring1.recv(0)
    ring1.start(1)
    core(1, 1, False).start()
    core(1, 3, False).start()
    assemble(dom_of(xh, y, c))
    assemble(dom_of(xh2, y, c))
    ring0.recv(1)
    core(0, 2, False).start()
    book_ring.recv(2)
    book_ring.start(3)
    for dy in (1, 3):
        assemble(dom_of(xh, turn(y, dy, y_n), c))
        assemble(dom_of(xh2, turn(y, dy, y_n), c))
    ring1.recv(1)
    core(1, 2, False).start()
    for j in range(2):
        assemble(dom_of(xh2 if j else xh, turn(y, 2, y_n), c))
    for dy in (0, 1, 3, 2):
        for j in range(2):
            core(j, dy, True).wait_recv()
            assemble(dom_of(xh2 if j else xh, turn(y, dy, y_n), turn(c, 1, c_n)))

    d_model = x_ref.shape[1]
    squares = jnp.zeros((1, 128), F32)
    for i in range(d_model // 256):
        enc = jnp.dot(x_ref[...], w_full[:, i * 256 : (i + 1) * 256], preferred_element_type=F32)
        for h in range(2):
            enc_t = enc[:, h * 128 : (h + 1) * 128].T
            squares = squares + jnp.sum(enc_t * enc_t, axis=0, keepdims=True)
            normed_t[i * 256 + h * 128 : i * 256 + (h + 1) * 128, :] = enc_t
    inv_rms = lax.rsqrt(squares / d_model + EPS)
    for i in range(d_model // 128):
        value = normed_t[i * 128 : (i + 1) * 128, :] * inv_rms
        normed_t[i * 128 : (i + 1) * 128, :] = value
        qs[z, i * 128 : (i + 1) * 128, :] = value.astype(BF16)

    half_d = d_model // 2
    q_ring = Ring(
        lambda i: qs.at[i],
        lambda i, h: qs.at[i, pl.ds(h * half_d, half_d)],
        z,
        z_n,
        lambda i: dev(z_=i),
        q_s,
        q_r,
    )
    q_ring.start(0)
    rebuild(turn(z, 2, z_n))
    rebuild(turn(z, -2, z_n))
    rebuild(turn(z, 3, z_n))
    rebuild(turn(z, -3, z_n))
    q_ring.recv(0)
    q_ring.start(1)
    book_ring.recv(3)
    rebuild(turn(z, 4, z_n))

    def flip(i, carry):
        f0 = pl.multiple_of(i * 128, 128)
        for t in range(n_pass // 128):
            pas[t * 128 : (t + 1) * 128, pl.ds(f0, 128)] = (
                pt[pl.ds(f0, 128), t * 128 : (t + 1) * 128].astype(F32).T.astype(BF16)
            )
        return carry

    lax.fori_loop(0, d_model // 128, flip, 0)

    sub8 = lax.broadcasted_iota(jnp.int32, (8, 128), 0)

    def score(j, totals):
        b = turn(z, j, z_n)
        block = qs[b]
        q_cat[:, j * 128 : (j + 1) * 128] = block
        total = jnp.zeros((1, 128), F32)
        for t in range(n_pass // 256):
            s = jnp.dot(pas[t * 256 : (t + 1) * 256, :], block, preferred_element_type=F32)
            e = jnp.exp(s)
            exps[j, t * 256 : (t + 1) * 256, :] = e
            total = total + jnp.sum(e, axis=0, keepdims=True)
        return totals + jnp.where(sub8 == b, jnp.broadcast_to(total, (8, 128)), 0.0)

    totals = score(0, jnp.zeros((8, 128), F32))
    totals = score(1, totals)
    totals = score(7, totals)
    q_ring.recv(1)
    q_ring.start(2)
    totals = score(2, totals)
    totals = score(6, totals)
    q_ring.recv(2)
    q_ring.start(3)
    totals = score(3, totals)
    totals = score(5, totals)
    q_ring.recv(3)
    totals = score(4, totals)

    tots[z] = totals

    def tot(d, back):
        other = turn(z, -d if back else d, z_n)
        ref = tots.at[other if back else z]
        return pltpu.make_async_remote_copy(
            src_ref=ref,
            dst_ref=ref,
            send_sem=tot_s.at[d - 1],
            recv_sem=tot_r.at[d - 1],
            device_id=dev(z_=other),
            device_id_type=MESH,
        )

    for d in range(1, z_n):
        tot(d, False).start()
    for d in range(1, z_n):
        tot(d, True).wait_recv()
    totals = tots[0]
    for i in range(1, z_n):
        totals = totals + tots[i]
    inverse = 1.0 / totals

    sub16 = lax.broadcasted_iota(jnp.int32, (16, 128), 0)
    first = z * n_pass
    weights_all, pos_all = wt_ref[...], pos_ref[...]

    def grads(j):
        b = turn(z, j, z_n)
        inv = jnp.sum(jnp.where(sub8 == b, inverse, 0.0), axis=0, keepdims=True)
        wt = jnp.sum(jnp.where(sub16 == b * x_n + x, weights_all, 0.0), axis=0, keepdims=True)
        pos = jnp.sum(jnp.where(sub16 == b * x_n + x, pos_all, 0), axis=0, keepdims=True) - first
        for t in range(n_pass // 256):
            e = exps[j, t * 256 : (t + 1) * 256, :]
            ids = lax.broadcasted_iota(jnp.int32, (256, 128), 0) + t * 256
            prob = e * inv
            gs_cat[t * 256 : (t + 1) * 256, j * 128 : (j + 1) * 128] = (
                wt * jnp.where(ids == pos, prob - 1.0, prob)
            ).astype(BF16)
        block = gs_cat[:, j * 128 : (j + 1) * 128]
        for t in range(d_model // 256):
            gn[j, t * 256 : (t + 1) * 256, :] = jnp.dot(
                pt[t * 256 : (t + 1) * 256, :], block, preferred_element_type=F32
            )

    order = [(4, 0), (3, 1), (3, 0), (2, 1), (2, 0), (1, 1), (1, 0)]

    def gn_copy(way, k):
        j, h = order[k]
        if way:
            j, h = z_n - j, 1 - h
        return pltpu.make_async_remote_copy(
            src_ref=gn.at[j, pl.ds(h * half_d, half_d)],
            dst_ref=slots.at[way, k],
            send_sem=gn_s.at[way, k],
            recv_sem=gn_r.at[way, k],
            device_id=dev(z_=turn(z, -1 if way else 1, z_n)),
            device_id_type=MESH,
        )

    def absorb(way, k):
        gn_copy(way, k).wait_recv()
        j, h = order[k]
        j -= 1
        if way:
            j, h = (z_n - j) % z_n, 1 - h
        gn[j, h * half_d : (h + 1) * half_d, :] += slots[way, k]

    grads(4)
    gn_copy(0, 0).start()
    gn_copy(1, 0).start()
    grads(3)
    gn_copy(0, 1).start()
    grads(5)
    gn_copy(1, 1).start()
    for way in range(2):
        absorb(way, 0)
        gn_copy(way, 2).start()
    grads(2)
    grads(6)
    for way in range(2):
        absorb(way, 1)
        gn_copy(way, 3).start()
    grads(1)
    grads(7)
    grads(0)

    def passage_grads(i, carry):
        p0 = pl.multiple_of(i * 256, 256)
        gpt[:, pl.ds(p0, 256)] = lax.dot_general(
            q_cat[...], gs_cat[pl.ds(p0, 256), :], NT, preferred_element_type=F32
        )
        return carry

    lax.fori_loop(0, n_pass // 256, passage_grads, 0)

    for way in range(2):
        absorb(way, 2)
        gn_copy(way, 4).start()

    levels = lax.broadcasted_iota(jnp.int32, (64, n_pass), 0).astype(BF16)

    def scatter(lo_m, hi_m):
        def per_sub(m, carry):
            r = pl.multiple_of(m * 8, 8)
            code = codes_t[pl.ds(m, 1), :]
            low = (code & 63).astype(BF16)
            high = jnp.broadcast_to(lax.shift_right_logical(code, 6).astype(BF16), (16, n_pass))
            g = gpt[pl.ds(r, 8), :]
            g_hi = g.astype(BF16).astype(F32)
            g16 = jnp.concatenate([g_hi, g - g_hi], 0).astype(BF16)
            left = jnp.concatenate([jnp.where(high == BF16(h), g16, BF16(0)) for h in range(4)], 0)
            onehot = jnp.where(levels == jnp.broadcast_to(low, (64, n_pass)), BF16(1), BF16(0))
            out = lax.dot_general(left, onehot, NT, preferred_element_type=F32)
            cg_ref[pl.ds(r, 8), :] = jnp.concatenate(
                [out[h * 16 : h * 16 + 8] + out[h * 16 + 8 : h * 16 + 16] for h in range(4)], 1
            )
            return carry

        lax.fori_loop(lo_m, hi_m, per_sub, 0)

    cut = n_sub // 4
    scatter(0, cut)
    for way in range(2):
        absorb(way, 3)
        gn_copy(way, 5).start()
    scatter(cut, 2 * cut)
    for way in range(2):
        absorb(way, 4)
        gn_copy(way, 6).start()
    scatter(2 * cut, 3 * cut)
    for way in range(2):
        absorb(way, 5)
    scatter(3 * cut, n_sub)
    for way in range(2):
        absorb(way, 6)

    inner = jnp.zeros((1, 128), F32)
    for i in range(d_model // 256):
        part = slice(i * 256, (i + 1) * 256)
        inner = inner + jnp.sum(gn[0, part, :] * normed_t[part, :], axis=0, keepdims=True)
    inner = inner / d_model
    for i in range(d_model // 256):
        part = slice(i * 256, (i + 1) * 256)
        ge = (inv_rms * (gn[0, part, :] - normed_t[part, :] * inner)).astype(BF16)
        wg_ref[:, part] = lax.dot_general(xt[...], ge, NT, preferred_element_type=F32)

    for i in range(len(in_group)):
        a1(i, False).wait_send()
    a2(False).wait_send()
    for ring in (ring0, ring1, book_ring, q_ring):
        ring.finish()
    for j in range(2):
        for dy in range(y_n):
            core(j, dy, False).wait_send()
    for d in range(1, z_n):
        tot(d, False).wait_send()
    for way in range(2):
        for k in range(len(order)):
            gn_copy(way, k).wait_send()


def per_device(sizes, queries_in, encoder_weight, codebook, codes, positive_ids, loss_weight):
    xh_n, y_n, c_n, z_n, x_n = sizes
    q_rows, d_model = queries_in.shape[1:]
    w_rows = encoder_weight.shape[0]
    subs, width, words = codebook.shape[1:]
    n_pass, n_sub = codes.shape[1:]
    blk = w_rows * d_model // 128
    group, doms = z_n * x_n, xh_n * y_n * c_n
    w = encoder_weight.reshape(w_rows, d_model // 128, 128).transpose(1, 0, 2).reshape(blk, 128)
    vmem = pl.BlockSpec(memory_space=pltpu.VMEM)
    dma = pltpu.SemaphoreType.DMA
    wg, cg = pl.pallas_call(
        functools.partial(kernel, sizes),
        out_shape=(
            jax.ShapeDtypeStruct((d_model, d_model), F32),
            jax.ShapeDtypeStruct((d_model, words), F32),
        ),
        in_specs=[vmem] * 6,
        out_specs=(vmem, vmem),
        scratch_shapes=[
            pltpu.VMEM((doms, group, blk, 128), BF16),
            pltpu.VMEM((d_model, d_model), BF16),
            pltpu.VMEM((d_model, q_rows), BF16),
            pltpu.VMEM((z_n, subs * width, words), BF16),
            pltpu.VMEM((n_sub, n_pass), jnp.int32),
            pltpu.VMEM((d_model, n_pass), BF16),
            pltpu.VMEM((n_pass, d_model), BF16),
            pltpu.VMEM((z_n, d_model, q_rows), BF16),
            pltpu.VMEM((d_model, z_n * q_rows), BF16),
            pltpu.VMEM((z_n, n_pass, q_rows), F32),
            pltpu.VMEM((n_pass, z_n * q_rows), BF16),
            pltpu.VMEM((z_n, d_model, q_rows), F32),
            pltpu.VMEM((2, 7, d_model // 2, q_rows), F32),
            pltpu.VMEM((d_model, n_pass), F32),
            pltpu.VMEM((d_model, q_rows), F32),
            pltpu.VMEM((z_n, 8, 128), F32),
            dma((group - 1,)),
            dma((group - 1,)),
            dma,
            dma,
            dma((2, 2, y_n // 2)),
            dma((2, 2, y_n // 2)),
            dma((2, y_n)),
            dma((2, y_n)),
            dma((2, z_n // 2)),
            dma((2, z_n // 2)),
            dma((2, z_n // 2)),
            dma((2, z_n // 2)),
            dma((z_n - 1,)),
            dma((z_n - 1,)),
            dma((2, 7)),
            dma((2, 7)),
        ],
        compiler_params=pltpu.CompilerParams(
            collective_id=0, has_side_effects=True, vmem_limit_bytes=60 * 2**20
        ),
        name="encoder_codebook_grads",
    )(
        w,
        queries_in[0],
        codebook.reshape(subs * width, words),
        codes[0],
        positive_ids.reshape(group, q_rows),
        loss_weight.reshape(group, q_rows).astype(F32),
    )
    book_grad = lax.psum_scatter(
        cg.reshape(n_sub, width, words), ("shard", "dp"), scatter_dimension=0, tiled=True
    )
    weight_grad = lax.psum_scatter(wg, ("dom", "shard", "dp"), scatter_dimension=0, tiled=True)
    return weight_grad, book_grad[None]


def solution(mesh):
    doms = mesh.shape["dom"]
    sizes = (2, doms // 4, 2, mesh.shape["shard"], mesh.shape["dp"])
    return jax.shard_map(
        functools.partial(per_device, sizes),
        mesh=mesh,
        in_specs=(
            P("dom", ("shard", "dp"), None),
            P(("dom", "shard", "dp"), None),
            P("dom", "shard", None, None),
            P("dom", "shard", None),
            P("dom", None),
            P("dom", None),
        ),
        out_specs=(P(("dom", "shard", "dp"), None), P("dom", ("shard", "dp"), None, None)),
        check_vma=False,
    )
```

```python
import functools

import jax
import jax.numpy as jnp
from jax import lax
from jax.experimental import pallas as pl
from jax.experimental.pallas import tpu as pltpu
from jax.sharding import PartitionSpec as P

MESH = pl.DeviceIdType.MESH
BF16 = jnp.bfloat16
F32 = jnp.float32
EPS = 1e-06
NT = (((1,), (1,)), ((), ()))


class Ring:
    def __init__(self, slot, half, me, n, dev, send_sem, recv_sem):
        self.slot, self.half, self.me, self.n, self.dev = slot, half, me, n, dev
        self.send_sem, self.recv_sem, self.k = send_sem, recv_sem, n // 2

    def at(self, offset):
        return lax.rem(self.me + offset + self.n, self.n)

    def copies(self, s, shift):
        views = (self.slot, self.slot) if s < self.k - 1 else (lambda i: self.half(i, 0), lambda i: self.half(i, 1))
        out = []
        for way, sign in ((0, 1), (1, -1)):
            ref = views[way](self.at(-sign * (s + shift)))
            out.append(
                pltpu.make_async_remote_copy(
                    src_ref=ref,
                    dst_ref=ref,
                    send_sem=self.send_sem.at[way, s],
                    recv_sem=self.recv_sem.at[way, s],
                    device_id=self.dev(self.at(sign)),
                    device_id_type=MESH,
                )
            )
        return out

    def start(self, s):
        for copy in self.copies(s, 0):
            copy.start()

    def recv(self, s):
        for copy in self.copies(s, 1):
            copy.wait_recv()

    def finish(self):
        for s in range(self.k):
            for copy in self.copies(s, 0):
                copy.wait_send()


class RingSum:
    def __init__(self, view, slots, n, right, left, send_sem, recv_sem):
        self.view, self.slots, self.n, self.to = view, slots, n, (right, left)
        self.send_sem, self.recv_sem = send_sem, recv_sem
        k = n // 2
        self.order = [(k, 0)] + [(j, h) for j in range(k - 1, 0, -1) for h in (1, 0)]

    def part(self, way, i, nearer):
        j, h = self.order[i]
        j -= nearer
        return self.view((self.n - j) % self.n, 1 - h) if way else self.view(j, h)

    def copy(self, way, i):
        return pltpu.make_async_remote_copy(
            src_ref=self.part(way, i, 0),
            dst_ref=self.slots.at[way, i],
            send_sem=self.send_sem.at[way, i],
            recv_sem=self.recv_sem.at[way, i],
            device_id=self.to[way],
            device_id_type=MESH,
        )

    def send(self, i):
        for way in range(2):
            self.copy(way, i).start()

    def absorb(self, i):
        for way in range(2):
            self.copy(way, i).wait_recv()
            part = self.part(way, i, 1)
            part[...] += self.slots[way, i]
            if i + 2 < len(self.order):
                self.copy(way, i + 2).start()

    def finish(self):
        for i in range(len(self.order)):
            for way in range(2):
                self.copy(way, i).wait_send()


def kernel(
    sizes,
    w_ref,
    x_ref,
    book_ref,
    codes_ref,
    pos_ref,
    wt_ref,
    wg_ref,
    cg_ref,
    g_all,
    w_full,
    xt,
    books,
    codes_t,
    pt,
    pas,
    qs,
    q_cat,
    exps,
    gs_cat,
    gn,
    slots,
    gpt,
    normed_t,
    tots,
    ge_t,
    cg,
    cg_x,
    cg_slots,
    wz,
    wy,
    wz_slots,
    wy_slots,
    wz_in,
    wy_in,
    total,
    final,
    a1_s,
    a1_r,
    a2_s,
    a2_r,
    y_s,
    y_r,
    core_s,
    core_r,
    book_s,
    book_r,
    q_s,
    q_r,
    tot_s,
    tot_r,
    gn_s,
    gn_r,
    cx_s,
    cx_r,
    cz_s,
    cz_r,
    wc_s,
    wc_r,
    wz_s,
    wz_r,
    wy_s,
    wy_r,
    wzy_s,
    wzy_r,
    wyz_s,
    wyz_r,
    fin_s,
    fin_r,
):
    xh_n, y_n, c_n, z_n, x_n = sizes
    dom, z, x = lax.axis_index("dom"), lax.axis_index("shard"), lax.axis_index("dp")
    xh, y, c = dom // (y_n * c_n), lax.rem(dom // c_n, y_n), lax.rem(dom, c_n)

    def dom_of(xh_, y_, c_):
        return (xh_ * y_n + y_) * c_n + c_

    def dev(dom_=None, z_=None, x_=None):
        return {
            "dom": dom if dom_ is None else dom_,
            "shard": z if z_ is None else z_,
            "dp": x if x_ is None else x_,
        }

    def turn(i, d, n):
        return lax.rem(i + d + n, n)

    in_group = [(dz, dx) for dz in range(z_n) for dx in range(x_n) if (dz, dx) != (0, 0)]
    pending = []
    peers = [dev(z_=turn(z, dz, z_n), x_=turn(x, dx, x_n)) for dz, dx in in_group]
    peers += [dev(dom_of(turn(xh, 1, xh_n), y, c)), dev(dom_of(turn(xh, 1, xh_n), y, c), x_=turn(x, 1, x_n))]
    peers += [dev(dom_of(xh, turn(y, dy, y_n), c)) for dy in range(1, y_n)]
    peers += [dev(dom_of(xh, y, turn(c, 1, c_n)))]
    barrier = pltpu.get_barrier_semaphore()
    for peer in peers:
        pl.semaphore_signal(barrier, inc=1, device_id=peer, device_id_type=MESH)

    mine = z * x_n + x
    g_all[dom, mine] = w_ref[...]
    books[z] = book_ref[...].astype(BF16)
    pl.semaphore_wait(barrier, len(peers))

    def a1(i, back):
        dz, dx = in_group[i]
        sign = -1 if back else 1
        z_, x_ = turn(z, sign * dz, z_n), turn(x, sign * dx, x_n)
        ref = g_all.at[dom, z_ * x_n + x_ if back else mine]
        return pltpu.make_async_remote_copy(
            src_ref=ref,
            dst_ref=ref,
            send_sem=a1_s.at[i],
            recv_sem=a1_r.at[i],
            device_id=dev(z_=z_, x_=x_),
            device_id_type=MESH,
        )

    for i in range(len(in_group)):
        a1(i, False).start()
        pending.append(a1(i, False).wait_send)
    book_ring = Ring(
        lambda i: books.at[i],
        lambda i, h: books.at[i, pl.ds(h * (books.shape[1] // 2), books.shape[1] // 2)],
        z,
        z_n,
        lambda i: dev(z_=i),
        book_s,
        book_r,
    )
    book_ring.start(0)
    pending.append(book_ring.finish)

    n_sub, n_pass = codes_t.shape
    for i in range(n_pass // 128):
        codes_t[:, i * 128 : (i + 1) * 128] = codes_ref[i * 128 : (i + 1) * 128, :].T
    for i in range(x_ref.shape[1] // 128):
        turned = x_ref[:, i * 128 : (i + 1) * 128].astype(F32).T.astype(BF16)
        for h in range(2):
            xt[h, i * 64 : (i + 1) * 64, :] = turned[h * 64 : (h + 1) * 64]

    for i in range(len(in_group)):
        a1(i, True).wait_recv()

    xh2 = turn(xh, 1, xh_n)

    def a2(back):
        ref = g_all.at[dom_of(xh2 if back else xh, y, c)]
        return pltpu.make_async_remote_copy(
            src_ref=ref,
            dst_ref=ref,
            send_sem=a2_s,
            recv_sem=a2_r,
            device_id=dev(dom_of(xh2, y, c)),
            device_id_type=MESH,
        )

    def y_ring(j, xh_):
        half = g_all.shape[1] // 2
        return Ring(
            lambda i: g_all.at[dom_of(xh_, i, c)],
            lambda i, h: g_all.at[dom_of(xh_, i, c), pl.ds(h * half, half)],
            y,
            y_n,
            lambda i: dev(dom_of(xh, i, c)),
            y_s.at[j],
            y_r.at[j],
        )

    def core(j, dy, back):
        ref = g_all.at[dom_of(xh2 if j else xh, turn(y, dy, y_n), turn(c, 1, c_n) if back else c)]
        return pltpu.make_async_remote_copy(
            src_ref=ref,
            dst_ref=ref,
            send_sem=core_s.at[j, dy],
            recv_sem=core_r.at[j, dy],
            device_id=dev(dom_of(xh, y, turn(c, 1, c_n))),
            device_id_type=MESH,
        )

    blk, col_blocks = w_ref.shape[0], x_ref.shape[1] // 128
    r_rows = blk // col_blocks
    per = 16 // r_rows
    rows = blk * per
    o = lax.broadcasted_iota(jnp.int32, (rows, rows), 0)
    j_ = lax.broadcasted_iota(jnp.int32, (rows, rows), 1)
    perm = (
        (j_ == (lax.rem(o, 16) // r_rows) * blk + (o // 16) * r_rows + lax.rem(o, r_rows)).astype(F32).astype(BF16)
    )

    def assemble(dom_):
        for t in range(g_all.shape[1] // per):
            part = jnp.dot(
                perm, g_all[dom_, t * per : (t + 1) * per].reshape(rows, 128), preferred_element_type=F32
            ).astype(BF16)
            row = pl.multiple_of((dom_ * (g_all.shape[1] // per) + t) * 16, 16)
            for cb in range(col_blocks):
                w_full[pl.ds(row, 16), cb * 128 : (cb + 1) * 128] = part[cb * 16 : (cb + 1) * 16]

    def rebuild(zb):
        groups = books.shape[1] // 64

        def per_group(gi, carry):
            r = pl.multiple_of(gi * 64, 64)
            table = books[zb, pl.ds(r, 64), :].astype(F32)
            out_row = pl.multiple_of(zb * books.shape[1] + r, 64)
            code_row = pl.multiple_of((zb * groups + gi) * 8, 8)

            def per_block(i, inner):
                for u in range(2):
                    p0 = pl.multiple_of(i * 256 + u * 128, 128)
                    cc = codes_t[pl.ds(code_row, 8), pl.ds(p0, 128)]
                    for jj in range(4):
                        parts = []
                        for j in (2 * jj, 2 * jj + 1):
                            idx = jnp.broadcast_to(cc[j : j + 1, :], (8, 128))
                            low = idx & 127
                            lo = jnp.take_along_axis(
                                table[j * 8 : j * 8 + 8, :128], low, axis=1, mode="promise_in_bounds"
                            )
                            hi = jnp.take_along_axis(
                                table[j * 8 : j * 8 + 8, 128:], low, axis=1, mode="promise_in_bounds"
                            )
                            parts.append(jnp.where(idx >= 128, hi, lo))
                        pt[pl.ds(pl.multiple_of(out_row + jj * 16, 16), 16), pl.ds(p0, 128)] = jnp.concatenate(
                            parts, 0
                        ).astype(BF16)
                return inner

            return lax.fori_loop(0, n_pass // 256, per_block, carry)

        lax.fori_loop(0, groups, per_group, 0)

    ring0, ring1 = y_ring(0, xh), y_ring(1, xh2)
    pending += [ring0.finish, ring1.finish, a2(False).wait_send]
    pending += [core(j, dy, False).wait_send for j in range(2) for dy in range(y_n)]
    a2(False).start()
    ring0.start(0)
    core(0, 0, False).start()
    rebuild(z)
    book_ring.recv(0)
    book_ring.start(1)
    a2(True).wait_recv()
    ring1.start(0)
    core(1, 0, False).start()
    rebuild(turn(z, 1, z_n))
    ring0.recv(0)
    ring0.start(1)
    core(0, 1, False).start()
    core(0, 3, False).start()
    rebuild(turn(z, -1, z_n))
    book_ring.recv(1)
    book_ring.start(2)
    ring1.recv(0)
    ring1.start(1)
    core(1, 1, False).start()
    core(1, 3, False).start()
    assemble(dom_of(xh, y, c))
    assemble(dom_of(xh2, y, c))
    ring0.recv(1)
    core(0, 2, False).start()
    book_ring.recv(2)
    book_ring.start(3)
    for dy in (1, 3):
        assemble(dom_of(xh, turn(y, dy, y_n), c))
        assemble(dom_of(xh2, turn(y, dy, y_n), c))
    ring1.recv(1)
    core(1, 2, False).start()
    for j in range(2):
        assemble(dom_of(xh2 if j else xh, turn(y, 2, y_n), c))
    for dy in (0, 1, 3, 2):
        for j in range(2):
            core(j, dy, True).wait_recv()
            assemble(dom_of(xh2 if j else xh, turn(y, dy, y_n), turn(c, 1, c_n)))

    d_model = x_ref.shape[1]
    squares = jnp.zeros((1, 128), F32)
    for i in range(d_model // 256):
        enc = jnp.dot(x_ref[...], w_full[:, i * 256 : (i + 1) * 256], preferred_element_type=F32)
        for h in range(2):
            enc_t = enc[:, h * 128 : (h + 1) * 128].T
            squares = squares + jnp.sum(enc_t * enc_t, axis=0, keepdims=True)
            normed_t[i * 256 + h * 128 : i * 256 + (h + 1) * 128, :] = enc_t
    inv_rms = lax.rsqrt(squares / d_model + EPS)
    for i in range(d_model // 128):
        value = normed_t[i * 128 : (i + 1) * 128, :] * inv_rms
        normed_t[i * 128 : (i + 1) * 128, :] = value
        qs[z, i * 128 : (i + 1) * 128, :] = value.astype(BF16)

    half_d = d_model // 2
    q_ring = Ring(
        lambda i: qs.at[i],
        lambda i, h: qs.at[i, pl.ds(h * half_d, half_d)],
        z,
        z_n,
        lambda i: dev(z_=i),
        q_s,
        q_r,
    )
    q_ring.start(0)
    pending.append(q_ring.finish)
    rebuild(turn(z, 2, z_n))
    rebuild(turn(z, -2, z_n))
    rebuild(turn(z, 3, z_n))
    rebuild(turn(z, -3, z_n))
    q_ring.recv(0)
    q_ring.start(1)
    book_ring.recv(3)
    rebuild(turn(z, 4, z_n))

    def flip(i, carry):
        f0 = pl.multiple_of(i * 128, 128)
        for t in range(n_pass // 128):
            pas[t * 128 : (t + 1) * 128, pl.ds(f0, 128)] = (
                pt[pl.ds(f0, 128), t * 128 : (t + 1) * 128].astype(F32).T.astype(BF16)
            )
        return carry

    lax.fori_loop(0, d_model // 128, flip, 0)

    sub8 = lax.broadcasted_iota(jnp.int32, (8, 128), 0)

    def score(j, totals):
        b = turn(z, j, z_n)
        block = qs[b]
        q_cat[:, j * 128 : (j + 1) * 128] = block
        total = jnp.zeros((1, 128), F32)
        for t in range(n_pass // 256):
            s = jnp.dot(pas[t * 256 : (t + 1) * 256, :], block, preferred_element_type=F32)
            e = jnp.exp(s)
            exps[j, t * 256 : (t + 1) * 256, :] = e
            total = total + jnp.sum(e, axis=0, keepdims=True)
        return totals + jnp.where(sub8 == b, jnp.broadcast_to(total, (8, 128)), 0.0)

    totals = score(0, jnp.zeros((8, 128), F32))
    totals = score(1, totals)
    totals = score(7, totals)
    q_ring.recv(1)
    q_ring.start(2)
    totals = score(2, totals)
    totals = score(6, totals)
    q_ring.recv(2)
    q_ring.start(3)
    totals = score(3, totals)
    totals = score(5, totals)
    q_ring.recv(3)
    totals = score(4, totals)

    tots[z] = totals

    def tot(d, back):
        other = turn(z, -d if back else d, z_n)
        ref = tots.at[other if back else z]
        return pltpu.make_async_remote_copy(
            src_ref=ref,
            dst_ref=ref,
            send_sem=tot_s.at[d - 1],
            recv_sem=tot_r.at[d - 1],
            device_id=dev(z_=other),
            device_id_type=MESH,
        )

    for d in range(1, z_n):
        tot(d, False).start()
        pending.append(tot(d, False).wait_send)
    for d in range(1, z_n):
        tot(d, True).wait_recv()
    totals = tots[0]
    for i in range(1, z_n):
        totals = totals + tots[i]
    inverse = 1.0 / totals

    sub16 = lax.broadcasted_iota(jnp.int32, (16, 128), 0)
    first = z * n_pass
    weights_all, pos_all = wt_ref[...], pos_ref[...]

    def grads(j):
        b = turn(z, j, z_n)
        inv = jnp.sum(jnp.where(sub8 == b, inverse, 0.0), axis=0, keepdims=True)
        wt = jnp.sum(jnp.where(sub16 == b * x_n + x, weights_all, 0.0), axis=0, keepdims=True)
        pos = jnp.sum(jnp.where(sub16 == b * x_n + x, pos_all, 0), axis=0, keepdims=True) - first
        for t in range(n_pass // 256):
            e = exps[j, t * 256 : (t + 1) * 256, :]
            ids = lax.broadcasted_iota(jnp.int32, (256, 128), 0) + t * 256
            prob = e * inv
            gs_cat[t * 256 : (t + 1) * 256, j * 128 : (j + 1) * 128] = (
                wt * jnp.where(ids == pos, prob - 1.0, prob)
            ).astype(BF16)
        block = gs_cat[:, j * 128 : (j + 1) * 128]
        for t in range(d_model // 256):
            gn[j, t * 256 : (t + 1) * 256, :] = jnp.dot(
                pt[t * 256 : (t + 1) * 256, :], block, preferred_element_type=F32
            )

    right, left = dev(z_=turn(z, 1, z_n)), dev(z_=turn(z, -1, z_n))
    gn_ring = RingSum(
        lambda j, h: gn.at[j, pl.ds(h * half_d, half_d)], slots, z_n, right, left, gn_s, gn_r
    )
    pending.append(gn_ring.finish)
    grads(4)
    gn_ring.send(0)
    grads(3)
    grads(5)
    gn_ring.send(1)
    gn_ring.absorb(0)
    grads(2)
    grads(6)
    gn_ring.absorb(1)
    grads(1)
    grads(7)
    grads(0)

    def passage_grads(i, carry):
        p0 = pl.multiple_of(i * 256, 256)
        gpt[:, pl.ds(p0, 256)] = lax.dot_general(
            q_cat[...], gs_cat[pl.ds(p0, 256), :], NT, preferred_element_type=F32
        )
        return carry

    lax.fori_loop(0, n_pass // 256, passage_grads, 0)

    gn_ring.absorb(2)

    levels = lax.broadcasted_iota(jnp.int32, (64, n_pass), 0).astype(BF16)

    def scatter(lo_m, hi_m):
        def per_sub(m, carry):
            r = pl.multiple_of(m * 8, 8)
            code = codes_t[pl.ds(m, 1), :]
            low = (code & 63).astype(BF16)
            high = jnp.broadcast_to(lax.shift_right_logical(code, 6).astype(BF16), (16, n_pass))
            g = gpt[pl.ds(r, 8), :]
            g_hi = g.astype(BF16).astype(F32)
            g16 = jnp.concatenate([g_hi, g - g_hi], 0).astype(BF16)
            left = jnp.concatenate([jnp.where(high == BF16(h), g16, BF16(0)) for h in range(4)], 0)
            onehot = jnp.where(levels == jnp.broadcast_to(low, (64, n_pass)), BF16(1), BF16(0))
            out = lax.dot_general(left, onehot, NT, preferred_element_type=F32)
            cg[pl.ds(r, 8), :] = jnp.concatenate(
                [out[h * 16 : h * 16 + 8] + out[h * 16 + 8 : h * 16 + 16] for h in range(4)], 1
            )
            return carry

        lax.fori_loop(lo_m, hi_m, per_sub, 0)

    own_rows = cg.shape[0] // (z_n * x_n)

    def own_words(zb, dp):
        return pl.ds(pl.multiple_of((zb * x_n + dp) * own_rows, own_rows), own_rows)

    def to_pair(zb):
        return pltpu.make_async_remote_copy(
            src_ref=cg.at[own_words(zb, turn(x, 1, x_n))],
            dst_ref=cg_x.at[zb],
            send_sem=cx_s.at[zb],
            recv_sem=cx_r.at[zb],
            device_id=dev(x_=turn(x, 1, x_n)),
            device_id_type=MESH,
        )

    cut = n_sub // 4
    for step in range(4):
        scatter(step * cut, (step + 1) * cut)
        for zb in range(step * z_n // 4, (step + 1) * z_n // 4):
            to_pair(zb).start()
            pending.append(to_pair(zb).wait_send)
        gn_ring.absorb(step + 3)

    inner = jnp.zeros((1, 128), F32)
    for i in range(d_model // 256):
        part = slice(i * 256, (i + 1) * 256)
        inner = inner + jnp.sum(gn[0, part, :] * normed_t[part, :], axis=0, keepdims=True)
    inner = inner / d_model
    for i in range(d_model // 256):
        part = slice(i * 256, (i + 1) * 256)
        ge_t[part, :] = (inv_rms * (gn[0, part, :] - normed_t[part, :] * inner)).astype(BF16)

    def share(i, core_, right_half):
        out = lax.dot_general(
            xt[core_], ge_t[half_d:, :] if right_half else ge_t[:half_d, :], NT, preferred_element_type=F32
        )
        for xh_ in range(xh_n):
            for y_ in range(y_n):
                for z_ in range(z_n):
                    tile = out[((xh_ * y_n + y_) * z_n + z_) * 8 : ((xh_ * y_n + y_) * z_n + z_) * 8 + 8]
                    if right_half:
                        wz[i, z_, xh_, y_] = tile
                    else:
                        wy[i, y_, xh_, z_] = tile

    sibling = turn(c, 1, c_n)

    def to_core(i):
        buf = (wz, wy)[i]
        return pltpu.make_async_remote_copy(
            src_ref=buf.at[1],
            dst_ref=buf.at[2],
            send_sem=wc_s.at[i],
            recv_sem=wc_r.at[i],
            device_id=dev(dom_of(xh, y, sibling)),
            device_id_type=MESH,
        )

    share(1, sibling, True)
    to_core(0).start()
    share(1, sibling, False)
    to_core(1).start()
    share(0, c, True)
    share(0, c, False)
    pending += [to_core(0).wait_send, to_core(1).wait_send]

    wz_ring = RingSum(
        lambda j, h: wz.at[0, turn(z, j, z_n), h], wz_slots, z_n, right, left, wz_s, wz_r
    )
    wy_ring = RingSum(
        lambda j, h: wy.at[0, turn(y, j, y_n), h],
        wy_slots,
        y_n,
        dev(dom_of(xh, turn(y, 1, y_n), c)),
        dev(dom_of(xh, turn(y, -1, y_n), c)),
        wy_s,
        wy_r,
    )

    def cg_half(j, h):
        row = (turn(z, j, z_n) * x_n + x) * own_rows + h * (own_rows // 2)
        return cg.at[pl.ds(pl.multiple_of(row, own_rows // 2), own_rows // 2)]

    cg_ring = RingSum(cg_half, cg_slots, z_n, right, left, cz_s, cz_r)
    pending += [wz_ring.finish, wy_ring.finish, cg_ring.finish]

    to_core(0).wait_recv()
    for i in range(z_n):
        wz[0, i] += wz[2, i]
    for i in range(2):
        wz_ring.send(i)
    to_core(1).wait_recv()
    for i in range(y_n):
        wy[0, i] += wy[2, i]
    for i in range(2):
        wy_ring.send(i)
    for zb in range(z_n):
        to_pair(zb).wait_recv()
        cg[own_words(zb, x), :] += cg_x[zb]
    for i in range(2):
        cg_ring.send(i)

    def wzy(d, back):
        other = turn(y, -d if back else d, y_n)
        return pltpu.make_async_remote_copy(
            src_ref=wz.at[0, z, :, other],
            dst_ref=wz_in.at[other if back else y],
            send_sem=wzy_s.at[d - 1],
            recv_sem=wzy_r.at[d - 1],
            device_id=dev(dom_of(xh, other, c)),
            device_id_type=MESH,
        )

    def wyz(d, back):
        other = turn(z, -d if back else d, z_n)
        return pltpu.make_async_remote_copy(
            src_ref=wy.at[0, y, :, other],
            dst_ref=wy_in.at[other if back else z],
            send_sem=wyz_s.at[d - 1],
            recv_sem=wyz_r.at[d - 1],
            device_id=dev(z_=other),
            device_id_type=MESH,
        )

    for i in range(3):
        wz_ring.absorb(i)
        cg_ring.absorb(i)
        wy_ring.absorb(i)
    for d in range(1, z_n):
        wyz(d, False).start()
        pending.append(wyz(d, False).wait_send)
    for i in range(3, 7):
        wz_ring.absorb(i)
        cg_ring.absorb(i)
    for d in range(1, y_n):
        wzy(d, False).start()
        pending.append(wzy(d, False).wait_send)
    wy_in[z] = wy[0, y, :, z]
    wz_in[y] = wz[0, z, :, y]
    cg_ref[...] = cg[own_words(z, x), :]
    for d in range(1, z_n):
        wyz(d, True).wait_recv()
    acc = wy_in[0]
    for i in range(1, z_n):
        acc = acc + wy_in[i]
    total[:, :, :half_d] = acc
    for d in range(1, y_n):
        wzy(d, True).wait_recv()
    acc = wz_in[0]
    for i in range(1, y_n):
        acc = acc + wz_in[i]
    total[:, :, half_d:] = acc

    def last(k):
        xh_, x_ = turn(xh, k // 2, xh_n), turn(x, k % 2, x_n)
        return pltpu.make_async_remote_copy(
            src_ref=total.at[xh_],
            dst_ref=final.at[k - 1],
            send_sem=fin_s.at[k - 1],
            recv_sem=fin_r.at[k - 1],
            device_id=dev(dom_of(xh_, y, c), x_=x_),
            device_id_type=MESH,
        )

    for k in range(1, 4):
        last(k).start()
        pending.append(last(k).wait_send)
    acc = total[xh]
    for k in range(1, 4):
        last(k).wait_recv()
        acc = acc + final[k - 1]
    wg_ref[...] = jnp.where(x == 0, acc[:4], acc[4:])

    for wait in pending:
        wait()


def per_device(sizes, queries_in, encoder_weight, codebook, codes, positive_ids, loss_weight):
    xh_n, y_n, c_n, z_n, x_n = sizes
    q_rows, d_model = queries_in.shape[1:]
    w_rows = encoder_weight.shape[0]
    subs, width, words = codebook.shape[1:]
    n_pass, n_sub = codes.shape[1:]
    blk = w_rows * d_model // 128
    group, doms, half = z_n * x_n, xh_n * y_n * c_n, d_model // 2
    w = encoder_weight.reshape(w_rows, d_model // 128, 128).transpose(1, 0, 2).reshape(blk, 128)
    vmem = pl.BlockSpec(memory_space=pltpu.VMEM)
    dma = pltpu.SemaphoreType.DMA
    wg, cg = pl.pallas_call(
        functools.partial(kernel, sizes),
        out_shape=(
            jax.ShapeDtypeStruct((w_rows, d_model), F32),
            jax.ShapeDtypeStruct((d_model // group, words), F32),
        ),
        in_specs=[vmem] * 6,
        out_specs=(vmem, vmem),
        scratch_shapes=[
            pltpu.VMEM((doms, group, blk, 128), BF16),
            pltpu.VMEM((d_model, d_model), BF16),
            pltpu.VMEM((2, d_model // 2, q_rows), BF16),
            pltpu.VMEM((z_n, subs * width, words), BF16),
            pltpu.VMEM((n_sub, n_pass), jnp.int32),
            pltpu.VMEM((d_model, n_pass), BF16),
            pltpu.VMEM((n_pass, d_model), BF16),
            pltpu.VMEM((z_n, d_model, q_rows), BF16),
            pltpu.VMEM((d_model, z_n * q_rows), BF16),
            pltpu.VMEM((z_n, n_pass, q_rows), F32),
            pltpu.VMEM((n_pass, z_n * q_rows), BF16),
            pltpu.VMEM((z_n, d_model, q_rows), F32),
            pltpu.VMEM((2, z_n - 1, half, q_rows), F32),
            pltpu.VMEM((d_model, n_pass), F32),
            pltpu.VMEM((d_model, q_rows), F32),
            pltpu.VMEM((z_n, 8, 128), F32),
            pltpu.VMEM((d_model, q_rows), BF16),
            pltpu.VMEM((d_model, words), F32),
            pltpu.VMEM((z_n, d_model // group, words), F32),
            pltpu.VMEM((2, z_n - 1, d_model // group // 2, words), F32),
            pltpu.VMEM((3, z_n, xh_n, y_n, 8, half), F32),
            pltpu.VMEM((3, y_n, xh_n, z_n, 8, half), F32),
            pltpu.VMEM((2, z_n - 1, y_n, 8, half), F32),
            pltpu.VMEM((2, y_n - 1, z_n, 8, half), F32),
            pltpu.VMEM((y_n, xh_n, 8, half), F32),
            pltpu.VMEM((z_n, xh_n, 8, half), F32),
            pltpu.VMEM((xh_n, 8, d_model), F32),
            pltpu.VMEM((3, 8, d_model), F32),
            dma((group - 1,)),
            dma((group - 1,)),
            dma,
            dma,
            dma((2, 2, y_n // 2)),
            dma((2, 2, y_n // 2)),
            dma((2, y_n)),
            dma((2, y_n)),
            dma((2, z_n // 2)),
            dma((2, z_n // 2)),
            dma((2, z_n // 2)),
            dma((2, z_n // 2)),
            dma((z_n - 1,)),
            dma((z_n - 1,)),
            dma((2, z_n - 1)),
            dma((2, z_n - 1)),
            dma((z_n,)),
            dma((z_n,)),
            dma((2, z_n - 1)),
            dma((2, z_n - 1)),
            dma((2,)),
            dma((2,)),
            dma((2, z_n - 1)),
            dma((2, z_n - 1)),
            dma((2, y_n - 1)),
            dma((2, y_n - 1)),
            dma((y_n - 1,)),
            dma((y_n - 1,)),
            dma((z_n - 1,)),
            dma((z_n - 1,)),
            dma((3,)),
            dma((3,)),
        ],
        compiler_params=pltpu.CompilerParams(
            collective_id=0, has_side_effects=True, vmem_limit_bytes=60 * 2**20
        ),
        name="encoder_codebook_grads",
    )(
        w,
        queries_in[0],
        codebook.reshape(subs * width, words),
        codes[0],
        positive_ids.reshape(group, q_rows),
        loss_weight.reshape(group, q_rows).astype(F32),
    )
    return wg, cg.reshape(1, n_sub // group, width, words)


def solution(mesh):
    doms = mesh.shape["dom"]
    sizes = (2, doms // 4, 2, mesh.shape["shard"], mesh.shape["dp"])
    return jax.shard_map(
        functools.partial(per_device, sizes),
        mesh=mesh,
        in_specs=(
            P("dom", ("shard", "dp"), None),
            P(("dom", "shard", "dp"), None),
            P("dom", "shard", None, None),
            P("dom", "shard", None),
            P("dom", None),
            P("dom", None),
        ),
        out_specs=(P(("dom", "shard", "dp"), None), P("dom", ("shard", "dp"), None, None)),
        check_vma=False,
    )
```

```python
import functools

import jax
import jax.numpy as jnp
from jax import lax
from jax.experimental import pallas as pl
from jax.experimental.pallas import tpu as pltpu
from jax.sharding import PartitionSpec as P

MESH = pl.DeviceIdType.MESH
BF16 = jnp.bfloat16
F32 = jnp.float32
EPS = 1e-06
NT = (((1,), (1,)), ((), ()))


class Ring:
    def __init__(self, slot, half, me, n, dev, send_sem, recv_sem):
        self.slot, self.half, self.me, self.n, self.dev = slot, half, me, n, dev
        self.send_sem, self.recv_sem, self.k = send_sem, recv_sem, n // 2

    def at(self, offset):
        return lax.rem(self.me + offset + self.n, self.n)

    def copies(self, s, shift):
        views = (self.slot, self.slot) if s < self.k - 1 else (lambda i: self.half(i, 0), lambda i: self.half(i, 1))
        out = []
        for way, sign in ((0, 1), (1, -1)):
            ref = views[way](self.at(-sign * (s + shift)))
            out.append(
                pltpu.make_async_remote_copy(
                    src_ref=ref,
                    dst_ref=ref,
                    send_sem=self.send_sem.at[way, s],
                    recv_sem=self.recv_sem.at[way, s],
                    device_id=self.dev(self.at(sign)),
                    device_id_type=MESH,
                )
            )
        return out

    def start(self, s):
        for copy in self.copies(s, 0):
            copy.start()

    def recv(self, s):
        for copy in self.copies(s, 1):
            copy.wait_recv()

    def finish(self):
        for s in range(self.k):
            for copy in self.copies(s, 0):
                copy.wait_send()


class RingSum:
    def __init__(self, view, bufs, n, right, left, send_sem, recv_sem):
        self.view, self.n, self.to = view, n, (right, left)
        self.out, self.out_step, self.slots, self.steps = bufs
        self.send_sem, self.recv_sem = send_sem, recv_sem
        k = n // 2
        self.order = [(k, 0)] + [(j, h) for j in range(k - 1, 0, -1) for h in (1, 0)]
        self.rows, self.lanes = self.out.shape[2:]
        self.tall = self.rows == 512

    def part(self, way, i, nearer):
        j, h = self.order[i]
        j -= nearer
        return self.view((self.n - j) % self.n, 1 - h) if way else self.view(j, h)

    def copies(self, way, i):
        return [
            pltpu.make_async_remote_copy(
                src_ref=src.at[way, i],
                dst_ref=dst.at[way, i],
                send_sem=self.send_sem.at[way, i, t],
                recv_sem=self.recv_sem.at[way, i, t],
                device_id=self.to[way],
                device_id_type=MESH,
            )
            for t, (src, dst) in enumerate(((self.out, self.slots), (self.out_step, self.steps)))
        ]

    def groups(self):
        return [(g, slice(g * 64, (g + 1) * 64)) for g in range(8)] if self.tall else [(0, slice(0, self.rows))]

    def start(self, way, i):
        part = self.part(way, i, 0)
        steps = []
        for _, rows in self.groups():
            value = part[rows, :] if self.tall else part[...].reshape(self.rows, self.lanes)
            largest = jnp.maximum(jnp.max(jnp.abs(value), axis=0, keepdims=True), 1e-30)
            self.out[way, i, rows, :] = jnp.round(value * (32767.0 / largest)).astype(jnp.int32).astype(jnp.int16)
            steps.append(largest * (1.0 / 32767.0))
        self.out_step[way, i] = (
            jnp.concatenate(steps, 0) if self.tall else jnp.broadcast_to(steps[0], (8, self.lanes))
        )
        for copy in self.copies(way, i):
            copy.start()

    def send(self, i):
        for way in range(2):
            self.start(way, i)

    def absorb(self, i):
        for way in range(2):
            for copy in self.copies(way, i):
                copy.wait_recv()
            part = self.part(way, i, 1)
            for g, rows in self.groups():
                value = self.slots[way, i, rows, :].astype(jnp.int32).astype(F32) * self.steps[way, i, g : g + 1, :]
                if self.tall:
                    part[rows, :] += value
                else:
                    part[...] += value.reshape(part.shape)
            if i + 2 < len(self.order):
                self.start(way, i + 2)

    def finish(self):
        for i in range(len(self.order)):
            for way in range(2):
                for copy in self.copies(way, i):
                    copy.wait_send()


def kernel(
    sizes,
    w_ref,
    x_ref,
    book_ref,
    codes_ref,
    pos_ref,
    wt_ref,
    wg_ref,
    cg_ref,
    g_all,
    w_full,
    xt,
    books,
    codes_t,
    pt,
    pas,
    qs,
    q_cat,
    exps,
    gs_cat,
    gn,
    gpt,
    normed_t,
    tots,
    ge_t,
    cg,
    cg_x,
    wz,
    wy,
    wz_in,
    wy_in,
    total,
    final,
    gn_out,
    gn_out_step,
    gn_in,
    gn_in_step,
    cg_out,
    cg_out_step,
    cg_in,
    cg_in_step,
    wz_out,
    wz_out_step,
    wz_got,
    wz_got_step,
    wy_out,
    wy_out_step,
    wy_got,
    wy_got_step,
    a1_s,
    a1_r,
    a2_s,
    a2_r,
    y_s,
    y_r,
    core_s,
    core_r,
    book_s,
    book_r,
    q_s,
    q_r,
    tot_s,
    tot_r,
    gn_s,
    gn_r,
    cx_s,
    cx_r,
    cz_s,
    cz_r,
    wc_s,
    wc_r,
    wz_s,
    wz_r,
    wy_s,
    wy_r,
    wzy_s,
    wzy_r,
    wyz_s,
    wyz_r,
    fin_s,
    fin_r,
):
    xh_n, y_n, c_n, z_n, x_n = sizes
    dom, z, x = lax.axis_index("dom"), lax.axis_index("shard"), lax.axis_index("dp")
    xh, y, c = dom // (y_n * c_n), lax.rem(dom // c_n, y_n), lax.rem(dom, c_n)

    def dom_of(xh_, y_, c_):
        return (xh_ * y_n + y_) * c_n + c_

    def dev(dom_=None, z_=None, x_=None):
        return {
            "dom": dom if dom_ is None else dom_,
            "shard": z if z_ is None else z_,
            "dp": x if x_ is None else x_,
        }

    def turn(i, d, n):
        return lax.rem(i + d + n, n)

    in_group = [(dz, dx) for dz in range(z_n) for dx in range(x_n) if (dz, dx) != (0, 0)]
    pending = []
    peers = [dev(z_=turn(z, dz, z_n), x_=turn(x, dx, x_n)) for dz, dx in in_group]
    peers += [dev(dom_of(turn(xh, 1, xh_n), y, c)), dev(dom_of(turn(xh, 1, xh_n), y, c), x_=turn(x, 1, x_n))]
    peers += [dev(dom_of(xh, turn(y, dy, y_n), c)) for dy in range(1, y_n)]
    peers += [dev(dom_of(xh, y, turn(c, 1, c_n)))]
    barrier = pltpu.get_barrier_semaphore()
    for peer in peers:
        pl.semaphore_signal(barrier, inc=1, device_id=peer, device_id_type=MESH)

    mine = z * x_n + x
    g_all[dom, mine] = w_ref[...]
    books[z] = book_ref[...].astype(BF16)
    pl.semaphore_wait(barrier, len(peers))

    def a1(i, back):
        dz, dx = in_group[i]
        sign = -1 if back else 1
        z_, x_ = turn(z, sign * dz, z_n), turn(x, sign * dx, x_n)
        ref = g_all.at[dom, z_ * x_n + x_ if back else mine]
        return pltpu.make_async_remote_copy(
            src_ref=ref,
            dst_ref=ref,
            send_sem=a1_s.at[i],
            recv_sem=a1_r.at[i],
            device_id=dev(z_=z_, x_=x_),
            device_id_type=MESH,
        )

    for i in range(len(in_group)):
        a1(i, False).start()
        pending.append(a1(i, False).wait_send)
    book_ring = Ring(
        lambda i: books.at[i],
        lambda i, h: books.at[i, pl.ds(h * (books.shape[1] // 2), books.shape[1] // 2)],
        z,
        z_n,
        lambda i: dev(z_=i),
        book_s,
        book_r,
    )
    book_ring.start(0)
    pending.append(book_ring.finish)

    n_sub, n_pass = codes_t.shape
    for i in range(n_pass // 128):
        codes_t[:, i * 128 : (i + 1) * 128] = codes_ref[i * 128 : (i + 1) * 128, :].T
    for i in range(x_ref.shape[1] // 128):
        turned = x_ref[:, i * 128 : (i + 1) * 128].astype(F32).T.astype(BF16)
        for h in range(2):
            xt[h, i * 64 : (i + 1) * 64, :] = turned[h * 64 : (h + 1) * 64]

    for i in range(len(in_group)):
        a1(i, True).wait_recv()

    xh2 = turn(xh, 1, xh_n)

    def a2(back):
        ref = g_all.at[dom_of(xh2 if back else xh, y, c)]
        return pltpu.make_async_remote_copy(
            src_ref=ref,
            dst_ref=ref,
            send_sem=a2_s,
            recv_sem=a2_r,
            device_id=dev(dom_of(xh2, y, c)),
            device_id_type=MESH,
        )

    def y_ring(j, xh_):
        half = g_all.shape[1] // 2
        return Ring(
            lambda i: g_all.at[dom_of(xh_, i, c)],
            lambda i, h: g_all.at[dom_of(xh_, i, c), pl.ds(h * half, half)],
            y,
            y_n,
            lambda i: dev(dom_of(xh, i, c)),
            y_s.at[j],
            y_r.at[j],
        )

    def core(j, dy, back):
        ref = g_all.at[dom_of(xh2 if j else xh, turn(y, dy, y_n), turn(c, 1, c_n) if back else c)]
        return pltpu.make_async_remote_copy(
            src_ref=ref,
            dst_ref=ref,
            send_sem=core_s.at[j, dy],
            recv_sem=core_r.at[j, dy],
            device_id=dev(dom_of(xh, y, turn(c, 1, c_n))),
            device_id_type=MESH,
        )

    blk, col_blocks = w_ref.shape[0], x_ref.shape[1] // 128
    r_rows = blk // col_blocks
    per = 16 // r_rows
    rows = blk * per
    o = lax.broadcasted_iota(jnp.int32, (rows, rows), 0)
    j_ = lax.broadcasted_iota(jnp.int32, (rows, rows), 1)
    perm = (
        (j_ == (lax.rem(o, 16) // r_rows) * blk + (o // 16) * r_rows + lax.rem(o, r_rows)).astype(F32).astype(BF16)
    )

    def assemble(dom_):
        for t in range(g_all.shape[1] // per):
            part = jnp.dot(
                perm, g_all[dom_, t * per : (t + 1) * per].reshape(rows, 128), preferred_element_type=F32
            ).astype(BF16)
            row = pl.multiple_of((dom_ * (g_all.shape[1] // per) + t) * 16, 16)
            for cb in range(col_blocks):
                w_full[pl.ds(row, 16), cb * 128 : (cb + 1) * 128] = part[cb * 16 : (cb + 1) * 16]

    def rebuild(zb):
        groups = books.shape[1] // 64

        def per_group(gi, carry):
            r = pl.multiple_of(gi * 64, 64)
            table = books[zb, pl.ds(r, 64), :].astype(F32)
            out_row = pl.multiple_of(zb * books.shape[1] + r, 64)
            code_row = pl.multiple_of((zb * groups + gi) * 8, 8)

            def per_block(i, inner):
                for u in range(2):
                    p0 = pl.multiple_of(i * 256 + u * 128, 128)
                    cc = codes_t[pl.ds(code_row, 8), pl.ds(p0, 128)]
                    for jj in range(4):
                        parts = []
                        for j in (2 * jj, 2 * jj + 1):
                            idx = jnp.broadcast_to(cc[j : j + 1, :], (8, 128))
                            low = idx & 127
                            lo = jnp.take_along_axis(
                                table[j * 8 : j * 8 + 8, :128], low, axis=1, mode="promise_in_bounds"
                            )
                            hi = jnp.take_along_axis(
                                table[j * 8 : j * 8 + 8, 128:], low, axis=1, mode="promise_in_bounds"
                            )
                            parts.append(jnp.where(idx >= 128, hi, lo))
                        pt[pl.ds(pl.multiple_of(out_row + jj * 16, 16), 16), pl.ds(p0, 128)] = jnp.concatenate(
                            parts, 0
                        ).astype(BF16)
                return inner

            return lax.fori_loop(0, n_pass // 256, per_block, carry)

        lax.fori_loop(0, groups, per_group, 0)

    ring0, ring1 = y_ring(0, xh), y_ring(1, xh2)
    pending += [ring0.finish, ring1.finish, a2(False).wait_send]
    pending += [core(j, dy, False).wait_send for j in range(2) for dy in range(y_n)]
    a2(False).start()
    ring0.start(0)
    core(0, 0, False).start()
    rebuild(z)
    book_ring.recv(0)
    book_ring.start(1)
    a2(True).wait_recv()
    ring1.start(0)
    core(1, 0, False).start()
    rebuild(turn(z, 1, z_n))
    ring0.recv(0)
    ring0.start(1)
    core(0, 1, False).start()
    core(0, 3, False).start()
    rebuild(turn(z, -1, z_n))
    book_ring.recv(1)
    book_ring.start(2)
    ring1.recv(0)
    ring1.start(1)
    core(1, 1, False).start()
    core(1, 3, False).start()
    assemble(dom_of(xh, y, c))
    assemble(dom_of(xh2, y, c))
    ring0.recv(1)
    core(0, 2, False).start()
    book_ring.recv(2)
    book_ring.start(3)
    for dy in (1, 3):
        assemble(dom_of(xh, turn(y, dy, y_n), c))
        assemble(dom_of(xh2, turn(y, dy, y_n), c))
    ring1.recv(1)
    core(1, 2, False).start()
    for j in range(2):
        assemble(dom_of(xh2 if j else xh, turn(y, 2, y_n), c))
    for dy in (0, 1, 3, 2):
        for j in range(2):
            core(j, dy, True).wait_recv()
            assemble(dom_of(xh2 if j else xh, turn(y, dy, y_n), turn(c, 1, c_n)))

    d_model = x_ref.shape[1]
    squares = jnp.zeros((1, 128), F32)
    for i in range(d_model // 256):
        enc = jnp.dot(x_ref[...], w_full[:, i * 256 : (i + 1) * 256], preferred_element_type=F32)
        for h in range(2):
            enc_t = enc[:, h * 128 : (h + 1) * 128].T
            squares = squares + jnp.sum(enc_t * enc_t, axis=0, keepdims=True)
            normed_t[i * 256 + h * 128 : i * 256 + (h + 1) * 128, :] = enc_t
    inv_rms = lax.rsqrt(squares / d_model + EPS)
    for i in range(d_model // 128):
        value = normed_t[i * 128 : (i + 1) * 128, :] * inv_rms
        normed_t[i * 128 : (i + 1) * 128, :] = value
        qs[z, i * 128 : (i + 1) * 128, :] = value.astype(BF16)

    half_d = d_model // 2
    q_ring = Ring(
        lambda i: qs.at[i],
        lambda i, h: qs.at[i, pl.ds(h * half_d, half_d)],
        z,
        z_n,
        lambda i: dev(z_=i),
        q_s,
        q_r,
    )
    q_ring.start(0)
    pending.append(q_ring.finish)
    rebuild(turn(z, 2, z_n))
    rebuild(turn(z, -2, z_n))
    rebuild(turn(z, 3, z_n))
    rebuild(turn(z, -3, z_n))
    q_ring.recv(0)
    q_ring.start(1)
    book_ring.recv(3)
    rebuild(turn(z, 4, z_n))

    def flip(i, carry):
        f0 = pl.multiple_of(i * 128, 128)
        for t in range(n_pass // 128):
            pas[t * 128 : (t + 1) * 128, pl.ds(f0, 128)] = (
                pt[pl.ds(f0, 128), t * 128 : (t + 1) * 128].astype(F32).T.astype(BF16)
            )
        return carry

    lax.fori_loop(0, d_model // 128, flip, 0)

    sub8 = lax.broadcasted_iota(jnp.int32, (8, 128), 0)

    def score(j, totals):
        b = turn(z, j, z_n)
        block = qs[b]
        q_cat[:, j * 128 : (j + 1) * 128] = block
        total = jnp.zeros((1, 128), F32)
        for t in range(n_pass // 256):
            s = jnp.dot(pas[t * 256 : (t + 1) * 256, :], block, preferred_element_type=F32)
            e = jnp.exp(s)
            exps[j, t * 256 : (t + 1) * 256, :] = e
            total = total + jnp.sum(e, axis=0, keepdims=True)
        return totals + jnp.where(sub8 == b, jnp.broadcast_to(total, (8, 128)), 0.0)

    totals = score(0, jnp.zeros((8, 128), F32))
    totals = score(1, totals)
    totals = score(7, totals)
    q_ring.recv(1)
    q_ring.start(2)
    totals = score(2, totals)
    totals = score(6, totals)
    q_ring.recv(2)
    q_ring.start(3)
    totals = score(3, totals)
    totals = score(5, totals)
    q_ring.recv(3)
    totals = score(4, totals)

    tots[z] = totals

    def tot(d, back):
        other = turn(z, -d if back else d, z_n)
        ref = tots.at[other if back else z]
        return pltpu.make_async_remote_copy(
            src_ref=ref,
            dst_ref=ref,
            send_sem=tot_s.at[d - 1],
            recv_sem=tot_r.at[d - 1],
            device_id=dev(z_=other),
            device_id_type=MESH,
        )

    for d in range(1, z_n):
        tot(d, False).start()
        pending.append(tot(d, False).wait_send)
    for d in range(1, z_n):
        tot(d, True).wait_recv()
    totals = tots[0]
    for i in range(1, z_n):
        totals = totals + tots[i]
    inverse = 1.0 / totals

    sub16 = lax.broadcasted_iota(jnp.int32, (16, 128), 0)
    first = z * n_pass
    weights_all, pos_all = wt_ref[...], pos_ref[...]

    def grads(j):
        b = turn(z, j, z_n)
        inv = jnp.sum(jnp.where(sub8 == b, inverse, 0.0), axis=0, keepdims=True)
        wt = jnp.sum(jnp.where(sub16 == b * x_n + x, weights_all, 0.0), axis=0, keepdims=True)
        pos = jnp.sum(jnp.where(sub16 == b * x_n + x, pos_all, 0), axis=0, keepdims=True) - first
        for t in range(n_pass // 256):
            e = exps[j, t * 256 : (t + 1) * 256, :]
            ids = lax.broadcasted_iota(jnp.int32, (256, 128), 0) + t * 256
            prob = e * inv
            gs_cat[t * 256 : (t + 1) * 256, j * 128 : (j + 1) * 128] = (
                wt * jnp.where(ids == pos, prob - 1.0, prob)
            ).astype(BF16)
        block = gs_cat[:, j * 128 : (j + 1) * 128]
        for t in range(d_model // 256):
            gn[j, t * 256 : (t + 1) * 256, :] = jnp.dot(
                pt[t * 256 : (t + 1) * 256, :], block, preferred_element_type=F32
            )

    right, left = dev(z_=turn(z, 1, z_n)), dev(z_=turn(z, -1, z_n))
    gn_ring = RingSum(
        lambda j, h: gn.at[j, pl.ds(h * half_d, half_d)], (gn_out, gn_out_step, gn_in, gn_in_step), z_n, right, left, gn_s, gn_r
    )
    pending.append(gn_ring.finish)
    grads(4)
    gn_ring.send(0)
    grads(3)
    grads(5)
    gn_ring.send(1)
    gn_ring.absorb(0)
    grads(2)
    grads(6)
    gn_ring.absorb(1)
    grads(1)
    grads(7)
    grads(0)

    def passage_grads(i, carry):
        p0 = pl.multiple_of(i * 256, 256)
        gpt[:, pl.ds(p0, 256)] = lax.dot_general(
            q_cat[...], gs_cat[pl.ds(p0, 256), :], NT, preferred_element_type=F32
        )
        return carry

    lax.fori_loop(0, n_pass // 256, passage_grads, 0)

    gn_ring.absorb(2)

    levels = lax.broadcasted_iota(jnp.int32, (64, n_pass), 0).astype(BF16)

    def scatter(lo_m, hi_m):
        def per_subs(i, carry):
            for u in range(4):
                m = i * 4 + u
                r = pl.multiple_of(m * 8, 8)
                code = codes_t[pl.ds(m, 1), :]
                low = (code & 63).astype(BF16)
                high = jnp.broadcast_to(lax.shift_right_logical(code, 6).astype(BF16), (16, n_pass))
                g = gpt[pl.ds(r, 8), :]
                g_hi = g.astype(BF16).astype(F32)
                g16 = jnp.concatenate([g_hi, g - g_hi], 0).astype(BF16)
                left = jnp.concatenate([jnp.where(high == BF16(h), g16, BF16(0)) for h in range(4)], 0)
                onehot = jnp.where(levels == jnp.broadcast_to(low, (64, n_pass)), BF16(1), BF16(0))
                out = lax.dot_general(left, onehot, NT, preferred_element_type=F32)
                cg[pl.ds(r, 8), :] = jnp.concatenate(
                    [out[h * 16 : h * 16 + 8] + out[h * 16 + 8 : h * 16 + 16] for h in range(4)], 1
                )
            return carry

        lax.fori_loop(lo_m // 4, hi_m // 4, per_subs, 0)

    own_rows = cg.shape[0] // (z_n * x_n)

    def own_words(zb, dp):
        return pl.ds(pl.multiple_of((zb * x_n + dp) * own_rows, own_rows), own_rows)

    def to_pair(zb):
        return pltpu.make_async_remote_copy(
            src_ref=cg.at[own_words(zb, turn(x, 1, x_n))],
            dst_ref=cg_x.at[zb],
            send_sem=cx_s.at[zb],
            recv_sem=cx_r.at[zb],
            device_id=dev(x_=turn(x, 1, x_n)),
            device_id_type=MESH,
        )

    def scatter_block(zb):
        scatter(zb * n_sub // z_n, (zb + 1) * n_sub // z_n)
        to_pair(zb).start()
        pending.append(to_pair(zb).wait_send)

    for zb in range(4):
        scatter_block(zb)
        gn_ring.absorb(zb + 3)

    inner = jnp.zeros((1, 128), F32)
    for i in range(d_model // 256):
        part = slice(i * 256, (i + 1) * 256)
        inner = inner + jnp.sum(gn[0, part, :] * normed_t[part, :], axis=0, keepdims=True)
    inner = inner / d_model
    for i in range(d_model // 256):
        part = slice(i * 256, (i + 1) * 256)
        ge_t[part, :] = (inv_rms * (gn[0, part, :] - normed_t[part, :] * inner)).astype(BF16)

    def share(i, core_, right_half):
        out = lax.dot_general(
            xt[core_], ge_t[half_d:, :] if right_half else ge_t[:half_d, :], NT, preferred_element_type=F32
        )
        for xh_ in range(xh_n):
            for y_ in range(y_n):
                for z_ in range(z_n):
                    tile = out[((xh_ * y_n + y_) * z_n + z_) * 8 : ((xh_ * y_n + y_) * z_n + z_) * 8 + 8]
                    if right_half:
                        wz[i, z_, xh_, y_] = tile
                    else:
                        wy[i, y_, xh_, z_] = tile

    sibling = turn(c, 1, c_n)

    def to_core(i):
        buf = (wz, wy)[i]
        return pltpu.make_async_remote_copy(
            src_ref=buf.at[1],
            dst_ref=buf.at[2],
            send_sem=wc_s.at[i],
            recv_sem=wc_r.at[i],
            device_id=dev(dom_of(xh, y, sibling)),
            device_id_type=MESH,
        )

    share(1, sibling, True)
    to_core(0).start()
    share(1, sibling, False)
    to_core(1).start()
    share(0, c, True)
    share(0, c, False)
    pending += [to_core(0).wait_send, to_core(1).wait_send]

    wz_ring = RingSum(
        lambda j, h: wz.at[0, turn(z, j, z_n), h], (wz_out, wz_out_step, wz_got, wz_got_step), z_n, right, left, wz_s, wz_r
    )
    wy_ring = RingSum(
        lambda j, h: wy.at[0, turn(y, j, y_n), h],
        (wy_out, wy_out_step, wy_got, wy_got_step),
        y_n,
        dev(dom_of(xh, turn(y, 1, y_n), c)),
        dev(dom_of(xh, turn(y, -1, y_n), c)),
        wy_s,
        wy_r,
    )

    def cg_half(j, h):
        row = (turn(z, j, z_n) * x_n + x) * own_rows + h * (own_rows // 2)
        return cg.at[pl.ds(pl.multiple_of(row, own_rows // 2), own_rows // 2)]

    cg_ring = RingSum(cg_half, (cg_out, cg_out_step, cg_in, cg_in_step), z_n, right, left, cz_s, cz_r)
    pending += [wz_ring.finish, wy_ring.finish, cg_ring.finish]

    to_core(0).wait_recv()
    for i in range(z_n):
        wz[0, i] += wz[2, i]
    for i in range(2):
        wz_ring.send(i)
    to_core(1).wait_recv()
    for i in range(y_n):
        wy[0, i] += wy[2, i]
    for i in range(2):
        wy_ring.send(i)
    def wzy(d, back):
        other = turn(y, -d if back else d, y_n)
        return pltpu.make_async_remote_copy(
            src_ref=wz.at[0, z, :, other],
            dst_ref=wz_in.at[other if back else y],
            send_sem=wzy_s.at[d - 1],
            recv_sem=wzy_r.at[d - 1],
            device_id=dev(dom_of(xh, other, c)),
            device_id_type=MESH,
        )

    def wyz(d, back):
        other = turn(z, -d if back else d, z_n)
        return pltpu.make_async_remote_copy(
            src_ref=wy.at[0, y, :, other],
            dst_ref=wy_in.at[other if back else z],
            send_sem=wyz_s.at[d - 1],
            recv_sem=wyz_r.at[d - 1],
            device_id=dev(z_=other),
            device_id_type=MESH,
        )

    for i in range(3):
        scatter_block(4 + i)
        wz_ring.absorb(i)
        wy_ring.absorb(i)
    for d in range(1, z_n):
        wyz(d, False).start()
        pending.append(wyz(d, False).wait_send)
    scatter_block(7)
    wz_ring.absorb(3)
    for zb in range(z_n):
        to_pair(zb).wait_recv()
        cg[own_words(zb, x), :] += cg_x[zb]
    for i in range(2):
        cg_ring.send(i)
    for i in range(3):
        wz_ring.absorb(4 + i)
        cg_ring.absorb(i)
    for d in range(1, y_n):
        wzy(d, False).start()
        pending.append(wzy(d, False).wait_send)
    wy_in[z] = wy[0, y, :, z]
    wz_in[y] = wz[0, z, :, y]
    cg_ring.absorb(3)
    for d in range(1, z_n):
        wyz(d, True).wait_recv()
    acc = wy_in[0]
    for i in range(1, z_n):
        acc = acc + wy_in[i]
    total[:, :, :half_d] = acc
    for d in range(1, y_n):
        wzy(d, True).wait_recv()
    acc = wz_in[0]
    for i in range(1, y_n):
        acc = acc + wz_in[i]
    total[:, :, half_d:] = acc

    def last(k):
        xh_, x_ = turn(xh, k // 2, xh_n), turn(x, k % 2, x_n)
        return pltpu.make_async_remote_copy(
            src_ref=total.at[xh_],
            dst_ref=final.at[k - 1],
            send_sem=fin_s.at[k - 1],
            recv_sem=fin_r.at[k - 1],
            device_id=dev(dom_of(xh_, y, c), x_=x_),
            device_id_type=MESH,
        )

    for k in range(1, 4):
        last(k).start()
        pending.append(last(k).wait_send)
    for i in range(4, 7):
        cg_ring.absorb(i)
    cg_ref[...] = cg[own_words(z, x), :]
    acc = total[xh]
    for k in range(1, 4):
        last(k).wait_recv()
        acc = acc + final[k - 1]
    wg_ref[...] = jnp.where(x == 0, acc[:4], acc[4:])

    for wait in pending:
        wait()


def per_device(sizes, queries_in, encoder_weight, codebook, codes, positive_ids, loss_weight):
    xh_n, y_n, c_n, z_n, x_n = sizes
    q_rows, d_model = queries_in.shape[1:]
    w_rows = encoder_weight.shape[0]
    subs, width, words = codebook.shape[1:]
    n_pass, n_sub = codes.shape[1:]
    blk = w_rows * d_model // 128
    group, doms, half = z_n * x_n, xh_n * y_n * c_n, d_model // 2
    w = encoder_weight.reshape(w_rows, d_model // 128, 128).transpose(1, 0, 2).reshape(blk, 128)

    def ring_bufs(n, rows, lanes):
        return 2 * [
            pltpu.VMEM((2, n - 1, rows, lanes), jnp.int16),
            pltpu.VMEM((2, n - 1, 8, lanes), F32),
        ]

    vmem = pl.BlockSpec(memory_space=pltpu.VMEM)
    dma = pltpu.SemaphoreType.DMA
    wg, cg = pl.pallas_call(
        functools.partial(kernel, sizes),
        out_shape=(
            jax.ShapeDtypeStruct((w_rows, d_model), F32),
            jax.ShapeDtypeStruct((d_model // group, words), F32),
        ),
        in_specs=[vmem] * 6,
        out_specs=(vmem, vmem),
        scratch_shapes=[
            pltpu.VMEM((doms, group, blk, 128), BF16),
            pltpu.VMEM((d_model, d_model), BF16),
            pltpu.VMEM((2, d_model // 2, q_rows), BF16),
            pltpu.VMEM((z_n, subs * width, words), BF16),
            pltpu.VMEM((n_sub, n_pass), jnp.int32),
            pltpu.VMEM((d_model, n_pass), BF16),
            pltpu.VMEM((n_pass, d_model), BF16),
            pltpu.VMEM((z_n, d_model, q_rows), BF16),
            pltpu.VMEM((d_model, z_n * q_rows), BF16),
            pltpu.VMEM((z_n, n_pass, q_rows), F32),
            pltpu.VMEM((n_pass, z_n * q_rows), BF16),
            pltpu.VMEM((z_n, d_model, q_rows), F32),
            pltpu.VMEM((d_model, n_pass), F32),
            pltpu.VMEM((d_model, q_rows), F32),
            pltpu.VMEM((z_n, 8, 128), F32),
            pltpu.VMEM((d_model, q_rows), BF16),
            pltpu.VMEM((d_model, words), F32),
            pltpu.VMEM((z_n, d_model // group, words), F32),
            pltpu.VMEM((3, z_n, xh_n, y_n, 8, half), F32),
            pltpu.VMEM((3, y_n, xh_n, z_n, 8, half), F32),
            pltpu.VMEM((y_n, xh_n, 8, half), F32),
            pltpu.VMEM((z_n, xh_n, 8, half), F32),
            pltpu.VMEM((xh_n, 8, d_model), F32),
            pltpu.VMEM((3, 8, d_model), F32),
            *ring_bufs(z_n, half, q_rows),
            *ring_bufs(z_n, d_model // group // 2, words),
            *ring_bufs(z_n, y_n * 8, half),
            *ring_bufs(y_n, z_n * 8, half),
            dma((group - 1,)),
            dma((group - 1,)),
            dma,
            dma,
            dma((2, 2, y_n // 2)),
            dma((2, 2, y_n // 2)),
            dma((2, y_n)),
            dma((2, y_n)),
            dma((2, z_n // 2)),
            dma((2, z_n // 2)),
            dma((2, z_n // 2)),
            dma((2, z_n // 2)),
            dma((z_n - 1,)),
            dma((z_n - 1,)),
            dma((2, z_n - 1, 2)),
            dma((2, z_n - 1, 2)),
            dma((z_n,)),
            dma((z_n,)),
            dma((2, z_n - 1, 2)),
            dma((2, z_n - 1, 2)),
            dma((2,)),
            dma((2,)),
            dma((2, z_n - 1, 2)),
            dma((2, z_n - 1, 2)),
            dma((2, y_n - 1, 2)),
            dma((2, y_n - 1, 2)),
            dma((y_n - 1,)),
            dma((y_n - 1,)),
            dma((z_n - 1,)),
            dma((z_n - 1,)),
            dma((3,)),
            dma((3,)),
        ],
        compiler_params=pltpu.CompilerParams(
            collective_id=0, has_side_effects=True, vmem_limit_bytes=60 * 2**20
        ),
        name="encoder_codebook_grads",
    )(
        w,
        queries_in[0],
        codebook.reshape(subs * width, words),
        codes[0],
        positive_ids.reshape(group, q_rows),
        loss_weight.reshape(group, q_rows).astype(F32),
    )
    return wg, cg.reshape(1, n_sub // group, width, words)


def solution(mesh):
    doms = mesh.shape["dom"]
    sizes = (2, doms // 4, 2, mesh.shape["shard"], mesh.shape["dp"])
    return jax.shard_map(
        functools.partial(per_device, sizes),
        mesh=mesh,
        in_specs=(
            P("dom", ("shard", "dp"), None),
            P(("dom", "shard", "dp"), None),
            P("dom", "shard", None, None),
            P("dom", "shard", None),
            P("dom", None),
            P("dom", None),
        ),
        out_specs=(P(("dom", "shard", "dp"), None), P("dom", ("shard", "dp"), None, None)),
        check_vma=False,
    )
```

```python
import functools

import jax
import jax.numpy as jnp
from jax import lax
from jax.experimental import pallas as pl
from jax.experimental.pallas import tpu as pltpu
from jax.sharding import PartitionSpec as P

MESH = pl.DeviceIdType.MESH
BF16 = jnp.bfloat16
F32 = jnp.float32
EPS = 1e-06
NT = (((1,), (1,)), ((), ()))


class Ring:
    def __init__(self, slot, half, me, n, dev, send_sem, recv_sem):
        self.slot, self.half, self.me, self.n, self.dev = slot, half, me, n, dev
        self.send_sem, self.recv_sem, self.k = send_sem, recv_sem, n // 2

    def at(self, offset):
        return lax.rem(self.me + offset + self.n, self.n)

    def copies(self, s, shift):
        views = (self.slot, self.slot) if s < self.k - 1 else (lambda i: self.half(i, 0), lambda i: self.half(i, 1))
        out = []
        for way, sign in ((0, 1), (1, -1)):
            ref = views[way](self.at(-sign * (s + shift)))
            out.append(
                pltpu.make_async_remote_copy(
                    src_ref=ref,
                    dst_ref=ref,
                    send_sem=self.send_sem.at[way, s],
                    recv_sem=self.recv_sem.at[way, s],
                    device_id=self.dev(self.at(sign)),
                    device_id_type=MESH,
                )
            )
        return out

    def start(self, s):
        for copy in self.copies(s, 0):
            copy.start()

    def recv(self, s):
        for copy in self.copies(s, 1):
            copy.wait_recv()

    def finish(self):
        for s in range(self.k):
            for copy in self.copies(s, 0):
                copy.wait_send()


class HalfRing:
    def __init__(self, half, me, n, right, left, send_sem, recv_sem):
        self.half, self.me, self.n, self.to = half, me, n, (right, left)
        self.send_sem, self.recv_sem = send_sem, recv_sem
        k = n // 2
        self.order = [(d, h) for d in range(k - 1) for h in (0, 1)] + [(k - 1, 0)]

    def copy(self, way, i, farther):
        d, h = self.order[i]
        d += farther
        ref = self.half(lax.rem(self.me + (d if way else self.n - d), self.n), 1 - h if way else h)
        return pltpu.make_async_remote_copy(
            src_ref=ref,
            dst_ref=ref,
            send_sem=self.send_sem.at[way, i],
            recv_sem=self.recv_sem.at[way, i],
            device_id=self.to[way],
            device_id_type=MESH,
        )

    def start(self, i):
        for way in range(2):
            self.copy(way, i, 0).start()

    def pass_on(self, i):
        for way in range(2):
            self.copy(way, i, 1).wait_recv()
            if i + 2 < len(self.order):
                self.copy(way, i + 2, 0).start()

    def finish(self):
        for i in range(len(self.order)):
            for way in range(2):
                self.copy(way, i, 0).wait_send()


class RingSum:
    def __init__(self, view, bufs, n, right, left, send_sem, recv_sem):
        self.view, self.n, self.to = view, n, (right, left)
        self.out, self.out_step, self.slots, self.steps = bufs
        self.send_sem, self.recv_sem = send_sem, recv_sem
        k = n // 2
        self.order = [(k, 0)] + [(j, h) for j in range(k - 1, 0, -1) for h in (1, 0)]
        self.rows, self.lanes = self.out.shape[2:]
        self.tall = self.rows == 512

    def part(self, way, i, nearer):
        j, h = self.order[i]
        j -= nearer
        return self.view((self.n - j) % self.n, 1 - h) if way else self.view(j, h)

    def copies(self, way, i):
        return [
            pltpu.make_async_remote_copy(
                src_ref=src.at[way, i],
                dst_ref=dst.at[way, i],
                send_sem=self.send_sem.at[way, i, t],
                recv_sem=self.recv_sem.at[way, i, t],
                device_id=self.to[way],
                device_id_type=MESH,
            )
            for t, (src, dst) in enumerate(((self.out, self.slots), (self.out_step, self.steps)))
        ]

    def groups(self):
        return [(g, slice(g * 64, (g + 1) * 64)) for g in range(8)] if self.tall else [(0, slice(0, self.rows))]

    def start(self, way, i):
        part = self.part(way, i, 0)
        steps = []
        for _, rows in self.groups():
            value = part[rows, :] if self.tall else part[...].reshape(self.rows, self.lanes)
            largest = jnp.maximum(jnp.max(jnp.abs(value), axis=0, keepdims=True), 1e-30)
            self.out[way, i, rows, :] = jnp.round(value * (32767.0 / largest)).astype(jnp.int32).astype(jnp.int16)
            steps.append(largest * (1.0 / 32767.0))
        self.out_step[way, i] = (
            jnp.concatenate(steps, 0) if self.tall else jnp.broadcast_to(steps[0], (8, self.lanes))
        )
        for copy in self.copies(way, i):
            copy.start()

    def send(self, i):
        for way in range(2):
            self.start(way, i)

    def absorb(self, i):
        for way in range(2):
            for copy in self.copies(way, i):
                copy.wait_recv()
            part = self.part(way, i, 1)
            for g, rows in self.groups():
                value = self.slots[way, i, rows, :].astype(jnp.int32).astype(F32) * self.steps[way, i, g : g + 1, :]
                if self.tall:
                    part[rows, :] += value
                else:
                    part[...] += value.reshape(part.shape)
            if i + 2 < len(self.order):
                self.start(way, i + 2)

    def finish(self):
        for i in range(len(self.order)):
            for way in range(2):
                for copy in self.copies(way, i):
                    copy.wait_send()


def kernel(
    sizes,
    w_ref,
    x_ref,
    book_ref,
    codes_ref,
    pos_ref,
    wt_ref,
    wg_ref,
    cg_ref,
    g_all,
    w_full,
    xt,
    books,
    codes_t,
    pt,
    pas,
    qs,
    q_cat,
    exps,
    gs_cat,
    gn,
    gpt,
    normed_t,
    tots,
    ge_t,
    cg,
    cg_x,
    wz,
    wy,
    wz_in,
    wy_in,
    total,
    final,
    gn_out,
    gn_out_step,
    gn_in,
    gn_in_step,
    cg_out,
    cg_out_step,
    cg_in,
    cg_in_step,
    wz_out,
    wz_out_step,
    wz_got,
    wz_got_step,
    wy_out,
    wy_out_step,
    wy_got,
    wy_got_step,
    a1_s,
    a1_r,
    a2_s,
    a2_r,
    y_s,
    y_r,
    core_s,
    core_r,
    book_s,
    book_r,
    q_s,
    q_r,
    tot_s,
    tot_r,
    gn_s,
    gn_r,
    cx_s,
    cx_r,
    cz_s,
    cz_r,
    wc_s,
    wc_r,
    wz_s,
    wz_r,
    wy_s,
    wy_r,
    wzy_s,
    wzy_r,
    wyz_s,
    wyz_r,
    fin_s,
    fin_r,
):
    xh_n, y_n, c_n, z_n, x_n = sizes
    dom, z, x = lax.axis_index("dom"), lax.axis_index("shard"), lax.axis_index("dp")
    xh, y, c = dom // (y_n * c_n), lax.rem(dom // c_n, y_n), lax.rem(dom, c_n)

    def dom_of(xh_, y_, c_):
        return (xh_ * y_n + y_) * c_n + c_

    def dev(dom_=None, z_=None, x_=None):
        return {
            "dom": dom if dom_ is None else dom_,
            "shard": z if z_ is None else z_,
            "dp": x if x_ is None else x_,
        }

    def turn(i, d, n):
        return lax.rem(i + d + n, n)

    pending = []
    peers = [dev(z_=turn(z, dz, z_n)) for dz in range(1, z_n)] + [dev(x_=turn(x, 1, x_n))]
    peers += [dev(dom_of(turn(xh, 1, xh_n), y, c)), dev(dom_of(turn(xh, 1, xh_n), y, c), x_=turn(x, 1, x_n))]
    peers += [dev(dom_of(xh, turn(y, dy, y_n), c)) for dy in range(1, y_n)]
    peers += [dev(dom_of(xh, y, turn(c, 1, c_n)))]
    barrier = pltpu.get_barrier_semaphore()
    for peer in peers:
        pl.semaphore_signal(barrier, inc=1, device_id=peer, device_id_type=MESH)

    mine = x * z_n + z
    g_all[dom, mine] = w_ref[...]
    books[z] = book_ref[...].astype(BF16)
    pl.semaphore_wait(barrier, len(peers))

    def a1(d, back):
        z_ = turn(z, -d if back else d, z_n)
        ref = g_all.at[dom, x * z_n + z_ if back else mine]
        return pltpu.make_async_remote_copy(
            src_ref=ref,
            dst_ref=ref,
            send_sem=a1_s.at[d - 1],
            recv_sem=a1_r.at[d - 1],
            device_id=dev(z_=z_),
            device_id_type=MESH,
        )

    for d in range(1, z_n):
        a1(d, False).start()
        pending.append(a1(d, False).wait_send)
    book_ring = Ring(
        lambda i: books.at[i],
        lambda i, h: books.at[i, pl.ds(h * (books.shape[1] // 2), books.shape[1] // 2)],
        z,
        z_n,
        lambda i: dev(z_=i),
        book_s,
        book_r,
    )
    book_ring.start(0)
    pending.append(book_ring.finish)

    n_sub, n_pass = codes_t.shape
    for i in range(n_pass // 128):
        codes_t[:, i * 128 : (i + 1) * 128] = codes_ref[i * 128 : (i + 1) * 128, :].T
    for i in range(x_ref.shape[1] // 128):
        turned = x_ref[:, i * 128 : (i + 1) * 128].astype(F32).T.astype(BF16)
        for h in range(2):
            xt[h, i * 64 : (i + 1) * 64, :] = turned[h * 64 : (h + 1) * 64]

    xh2, x2 = turn(xh, 1, xh_n), turn(x, 1, x_n)

    def a2(k, back):
        dom_, x_ = dom_of(xh2 if k // 2 else xh, y, c), x2 if k % 2 else x
        ref = g_all.at[dom_ if back else dom, pl.ds((x_ if back else x) * z_n, z_n)]
        return pltpu.make_async_remote_copy(
            src_ref=ref,
            dst_ref=ref,
            send_sem=a2_s.at[k - 1],
            recv_sem=a2_r.at[k - 1],
            device_id=dev(dom_, x_=x_),
            device_id_type=MESH,
        )

    for d in range(1, z_n):
        a1(d, True).wait_recv()
    for k in range(1, 4):
        a2(k, False).start()
        pending.append(a2(k, False).wait_send)

    def y_ring(j, xh_):
        half = g_all.shape[1] // 2
        return Ring(
            lambda i: g_all.at[dom_of(xh_, i, c)],
            lambda i, h: g_all.at[dom_of(xh_, i, c), pl.ds(h * half, half)],
            y,
            y_n,
            lambda i: dev(dom_of(xh, i, c)),
            y_s.at[j],
            y_r.at[j],
        )

    def core(j, dy, back):
        ref = g_all.at[dom_of(xh2 if j else xh, turn(y, dy, y_n), turn(c, 1, c_n) if back else c)]
        return pltpu.make_async_remote_copy(
            src_ref=ref,
            dst_ref=ref,
            send_sem=core_s.at[j, dy],
            recv_sem=core_r.at[j, dy],
            device_id=dev(dom_of(xh, y, turn(c, 1, c_n))),
            device_id_type=MESH,
        )

    blk, col_blocks = w_ref.shape[0], x_ref.shape[1] // 128
    r_rows = blk // col_blocks
    per = 16 // r_rows
    rows = blk * per
    o = lax.broadcasted_iota(jnp.int32, (rows, rows), 0)
    j_ = lax.broadcasted_iota(jnp.int32, (rows, rows), 1)
    perm = (
        (j_ == (lax.rem(o, 16) // r_rows) * blk + (o // 16) * r_rows + lax.rem(o, r_rows)).astype(F32).astype(BF16)
    )

    def assemble(dom_):
        for t in range(g_all.shape[1] // per):
            blocks = [g_all[dom_, (b % x_n) * z_n + b // x_n] for b in range(t * per, (t + 1) * per)]
            part = jnp.dot(perm, jnp.concatenate(blocks, 0), preferred_element_type=F32).astype(BF16)
            row = pl.multiple_of((dom_ * (g_all.shape[1] // per) + t) * 16, 16)
            for cb in range(col_blocks):
                w_full[pl.ds(row, 16), cb * 128 : (cb + 1) * 128] = part[cb * 16 : (cb + 1) * 16]

    def rebuild(zb):
        groups = books.shape[1] // 64

        def per_group(gi, carry):
            r = pl.multiple_of(gi * 64, 64)
            table = books[zb, pl.ds(r, 64), :].astype(F32)
            out_row = pl.multiple_of(zb * books.shape[1] + r, 64)
            code_row = pl.multiple_of((zb * groups + gi) * 8, 8)

            def per_block(i, inner):
                for u in range(2):
                    p0 = pl.multiple_of(i * 256 + u * 128, 128)
                    cc = codes_t[pl.ds(code_row, 8), pl.ds(p0, 128)]
                    for jj in range(4):
                        parts = []
                        for j in (2 * jj, 2 * jj + 1):
                            idx = jnp.broadcast_to(cc[j : j + 1, :], (8, 128))
                            low = idx & 127
                            lo = jnp.take_along_axis(
                                table[j * 8 : j * 8 + 8, :128], low, axis=1, mode="promise_in_bounds"
                            )
                            hi = jnp.take_along_axis(
                                table[j * 8 : j * 8 + 8, 128:], low, axis=1, mode="promise_in_bounds"
                            )
                            parts.append(jnp.where(idx >= 128, hi, lo))
                        pt[pl.ds(pl.multiple_of(out_row + jj * 16, 16), 16), pl.ds(p0, 128)] = jnp.concatenate(
                            parts, 0
                        ).astype(BF16)
                return inner

            return lax.fori_loop(0, n_pass // 256, per_block, carry)

        lax.fori_loop(0, groups, per_group, 0)

    ring0, ring1 = y_ring(0, xh), y_ring(1, xh2)
    pending += [ring0.finish, ring1.finish]
    pending += [core(j, dy, False).wait_send for j in range(2) for dy in range(y_n)]
    a2(1, True).wait_recv()
    ring0.start(0)
    core(0, 0, False).start()
    a2(2, True).wait_recv()
    a2(3, True).wait_recv()
    ring1.start(0)
    core(1, 0, False).start()
    rebuild(z)
    book_ring.recv(0)
    book_ring.start(1)
    rebuild(turn(z, 1, z_n))
    ring0.recv(0)
    ring0.start(1)
    core(0, 1, False).start()
    core(0, 3, False).start()
    rebuild(turn(z, -1, z_n))
    book_ring.recv(1)
    book_ring.start(2)
    ring1.recv(0)
    ring1.start(1)
    core(1, 1, False).start()
    core(1, 3, False).start()
    assemble(dom_of(xh, y, c))
    assemble(dom_of(xh2, y, c))
    ring0.recv(1)
    core(0, 2, False).start()
    book_ring.recv(2)
    book_ring.start(3)
    for dy in (1, 3):
        assemble(dom_of(xh, turn(y, dy, y_n), c))
        assemble(dom_of(xh2, turn(y, dy, y_n), c))
    ring1.recv(1)
    core(1, 2, False).start()
    for j in range(2):
        assemble(dom_of(xh2 if j else xh, turn(y, 2, y_n), c))
    for dy in (0, 1, 3, 2):
        for j in range(2):
            core(j, dy, True).wait_recv()
            assemble(dom_of(xh2 if j else xh, turn(y, dy, y_n), turn(c, 1, c_n)))

    d_model = x_ref.shape[1]
    squares = jnp.zeros((1, 128), F32)
    for i in range(d_model // 256):
        enc = jnp.dot(x_ref[...], w_full[:, i * 256 : (i + 1) * 256], preferred_element_type=F32)
        for h in range(2):
            enc_t = enc[:, h * 128 : (h + 1) * 128].T
            squares = squares + jnp.sum(enc_t * enc_t, axis=0, keepdims=True)
            normed_t[i * 256 + h * 128 : i * 256 + (h + 1) * 128, :] = enc_t
    inv_rms = lax.rsqrt(squares / d_model + EPS)
    for i in range(d_model // 128):
        value = normed_t[i * 128 : (i + 1) * 128, :] * inv_rms
        normed_t[i * 128 : (i + 1) * 128, :] = value
        qs[z, i * 128 : (i + 1) * 128, :] = value.astype(BF16)

    half_d = d_model // 2
    right, left = dev(z_=turn(z, 1, z_n)), dev(z_=turn(z, -1, z_n))
    q_ring = HalfRing(lambda i, h: qs.at[i, pl.ds(h * half_d, half_d)], z, z_n, right, left, q_s, q_r)
    q_ring.start(0)
    q_ring.start(1)
    pending.append(q_ring.finish)
    rebuild(turn(z, 2, z_n))
    rebuild(turn(z, -2, z_n))
    q_ring.pass_on(0)
    rebuild(turn(z, 3, z_n))
    rebuild(turn(z, -3, z_n))
    q_ring.pass_on(1)
    book_ring.recv(3)
    rebuild(turn(z, 4, z_n))
    q_ring.pass_on(2)

    def flip(i, carry):
        f0 = pl.multiple_of(i * 128, 128)
        for t in range(n_pass // 128):
            pas[t * 128 : (t + 1) * 128, pl.ds(f0, 128)] = (
                pt[pl.ds(f0, 128), t * 128 : (t + 1) * 128].astype(F32).T.astype(BF16)
            )
        return carry

    lax.fori_loop(0, d_model // 128, flip, 0)

    sub8 = lax.broadcasted_iota(jnp.int32, (8, 128), 0)

    def score(j, totals):
        b = turn(z, j, z_n)
        block = qs[b]
        q_cat[:, j * 128 : (j + 1) * 128] = block
        total = jnp.zeros((1, 128), F32)
        for t in range(n_pass // 256):
            s = jnp.dot(pas[t * 256 : (t + 1) * 256, :], block, preferred_element_type=F32)
            e = jnp.exp(s)
            exps[j, t * 256 : (t + 1) * 256, :] = e
            total = total + jnp.sum(e, axis=0, keepdims=True)
        return totals + jnp.where(sub8 == b, jnp.broadcast_to(total, (8, 128)), 0.0)

    totals = score(0, jnp.zeros((8, 128), F32))
    q_ring.pass_on(3)
    totals = score(1, totals)
    totals = score(7, totals)
    q_ring.pass_on(4)
    totals = score(2, totals)
    totals = score(6, totals)
    q_ring.pass_on(5)
    totals = score(3, totals)
    totals = score(5, totals)
    q_ring.pass_on(6)
    totals = score(4, totals)

    tots[z] = totals

    def tot(d, back):
        other = turn(z, -d if back else d, z_n)
        ref = tots.at[other if back else z]
        return pltpu.make_async_remote_copy(
            src_ref=ref,
            dst_ref=ref,
            send_sem=tot_s.at[d - 1],
            recv_sem=tot_r.at[d - 1],
            device_id=dev(z_=other),
            device_id_type=MESH,
        )

    for d in range(1, z_n):
        tot(d, False).start()
        pending.append(tot(d, False).wait_send)
    for d in range(1, z_n):
        tot(d, True).wait_recv()
    totals = tots[0]
    for i in range(1, z_n):
        totals = totals + tots[i]
    inverse = 1.0 / totals

    sub16 = lax.broadcasted_iota(jnp.int32, (16, 128), 0)
    first = z * n_pass
    weights_all, pos_all = wt_ref[...], pos_ref[...]

    def grads(j):
        b = turn(z, j, z_n)
        inv = jnp.sum(jnp.where(sub8 == b, inverse, 0.0), axis=0, keepdims=True)
        wt = jnp.sum(jnp.where(sub16 == b * x_n + x, weights_all, 0.0), axis=0, keepdims=True)
        pos = jnp.sum(jnp.where(sub16 == b * x_n + x, pos_all, 0), axis=0, keepdims=True) - first
        for t in range(n_pass // 256):
            e = exps[j, t * 256 : (t + 1) * 256, :]
            ids = lax.broadcasted_iota(jnp.int32, (256, 128), 0) + t * 256
            prob = e * inv
            gs_cat[t * 256 : (t + 1) * 256, j * 128 : (j + 1) * 128] = (
                wt * jnp.where(ids == pos, prob - 1.0, prob)
            ).astype(BF16)
        block = gs_cat[:, j * 128 : (j + 1) * 128]
        for t in range(d_model // 256):
            gn[j, t * 256 : (t + 1) * 256, :] = jnp.dot(
                pt[t * 256 : (t + 1) * 256, :], block, preferred_element_type=F32
            )

    gn_ring = RingSum(
        lambda j, h: gn.at[j, pl.ds(h * half_d, half_d)], (gn_out, gn_out_step, gn_in, gn_in_step), z_n, right, left, gn_s, gn_r
    )
    pending.append(gn_ring.finish)
    grads(4)
    gn_ring.send(0)
    grads(3)
    grads(5)
    gn_ring.send(1)
    gn_ring.absorb(0)
    grads(2)
    grads(6)
    gn_ring.absorb(1)
    grads(1)
    grads(7)
    grads(0)

    def passage_grads(i, carry):
        p0 = pl.multiple_of(i * 256, 256)
        gpt[:, pl.ds(p0, 256)] = lax.dot_general(
            q_cat[...], gs_cat[pl.ds(p0, 256), :], NT, preferred_element_type=F32
        )
        return carry

    lax.fori_loop(0, n_pass // 256, passage_grads, 0)

    gn_ring.absorb(2)

    levels = lax.broadcasted_iota(jnp.int32, (64, n_pass), 0).astype(BF16)

    def scatter(lo_m, hi_m):
        def per_subs(i, carry):
            for u in range(4):
                m = i * 4 + u
                r = pl.multiple_of(m * 8, 8)
                code = codes_t[pl.ds(m, 1), :]
                low = (code & 63).astype(BF16)
                high = jnp.broadcast_to(lax.shift_right_logical(code, 6).astype(BF16), (16, n_pass))
                g = gpt[pl.ds(r, 8), :]
                g_hi = g.astype(BF16).astype(F32)
                g16 = jnp.concatenate([g_hi, g - g_hi], 0).astype(BF16)
                left = jnp.concatenate([jnp.where(high == BF16(h), g16, BF16(0)) for h in range(4)], 0)
                onehot = jnp.where(levels == jnp.broadcast_to(low, (64, n_pass)), BF16(1), BF16(0))
                out = lax.dot_general(left, onehot, NT, preferred_element_type=F32)
                cg[pl.ds(r, 8), :] = jnp.concatenate(
                    [out[h * 16 : h * 16 + 8] + out[h * 16 + 8 : h * 16 + 16] for h in range(4)], 1
                )
            return carry

        lax.fori_loop(lo_m // 4, hi_m // 4, per_subs, 0)

    own_rows = cg.shape[0] // (z_n * x_n)

    def own_words(zb, dp):
        return pl.ds(pl.multiple_of((zb * x_n + dp) * own_rows, own_rows), own_rows)

    def to_pair(zb):
        return pltpu.make_async_remote_copy(
            src_ref=cg.at[own_words(zb, turn(x, 1, x_n))],
            dst_ref=cg_x.at[zb],
            send_sem=cx_s.at[zb],
            recv_sem=cx_r.at[zb],
            device_id=dev(x_=turn(x, 1, x_n)),
            device_id_type=MESH,
        )

    def scatter_block(zb):
        scatter(zb * n_sub // z_n, (zb + 1) * n_sub // z_n)
        to_pair(zb).start()
        pending.append(to_pair(zb).wait_send)

    for zb in range(4):
        scatter_block(zb)
        gn_ring.absorb(zb + 3)

    inner = jnp.zeros((1, 128), F32)
    for i in range(d_model // 256):
        part = slice(i * 256, (i + 1) * 256)
        inner = inner + jnp.sum(gn[0, part, :] * normed_t[part, :], axis=0, keepdims=True)
    inner = inner / d_model
    for i in range(d_model // 256):
        part = slice(i * 256, (i + 1) * 256)
        ge_t[part, :] = (inv_rms * (gn[0, part, :] - normed_t[part, :] * inner)).astype(BF16)

    def share(i, core_, right_half):
        out = lax.dot_general(
            xt[core_], ge_t[half_d:, :] if right_half else ge_t[:half_d, :], NT, preferred_element_type=F32
        )
        for xh_ in range(xh_n):
            for y_ in range(y_n):
                for z_ in range(z_n):
                    tile = out[((xh_ * y_n + y_) * z_n + z_) * 8 : ((xh_ * y_n + y_) * z_n + z_) * 8 + 8]
                    if right_half:
                        wz[i, z_, xh_, y_] = tile
                    else:
                        wy[i, y_, xh_, z_] = tile

    sibling = turn(c, 1, c_n)

    def to_core(i):
        buf = (wz, wy)[i]
        return pltpu.make_async_remote_copy(
            src_ref=buf.at[1],
            dst_ref=buf.at[2],
            send_sem=wc_s.at[i],
            recv_sem=wc_r.at[i],
            device_id=dev(dom_of(xh, y, sibling)),
            device_id_type=MESH,
        )

    share(1, sibling, True)
    to_core(0).start()
    share(1, sibling, False)
    to_core(1).start()
    share(0, c, True)
    share(0, c, False)
    pending += [to_core(0).wait_send, to_core(1).wait_send]

    wz_ring = RingSum(
        lambda j, h: wz.at[0, turn(z, j, z_n), h], (wz_out, wz_out_step, wz_got, wz_got_step), z_n, right, left, wz_s, wz_r
    )
    wy_ring = RingSum(
        lambda j, h: wy.at[0, turn(y, j, y_n), h],
        (wy_out, wy_out_step, wy_got, wy_got_step),
        y_n,
        dev(dom_of(xh, turn(y, 1, y_n), c)),
        dev(dom_of(xh, turn(y, -1, y_n), c)),
        wy_s,
        wy_r,
    )

    def cg_half(j, h):
        row = (turn(z, j, z_n) * x_n + x) * own_rows + h * (own_rows // 2)
        return cg.at[pl.ds(pl.multiple_of(row, own_rows // 2), own_rows // 2)]

    cg_ring = RingSum(cg_half, (cg_out, cg_out_step, cg_in, cg_in_step), z_n, right, left, cz_s, cz_r)
    pending += [wz_ring.finish, wy_ring.finish, cg_ring.finish]

    to_core(0).wait_recv()
    for i in range(z_n):
        wz[0, i] += wz[2, i]
    for i in range(2):
        wz_ring.send(i)
    to_core(1).wait_recv()
    for i in range(y_n):
        wy[0, i] += wy[2, i]
    for i in range(2):
        wy_ring.send(i)
    def wzy(d, back):
        other = turn(y, -d if back else d, y_n)
        return pltpu.make_async_remote_copy(
            src_ref=wz.at[0, z, :, other],
            dst_ref=wz_in.at[other if back else y],
            send_sem=wzy_s.at[d - 1],
            recv_sem=wzy_r.at[d - 1],
            device_id=dev(dom_of(xh, other, c)),
            device_id_type=MESH,
        )

    def wyz(d, back):
        other = turn(z, -d if back else d, z_n)
        return pltpu.make_async_remote_copy(
            src_ref=wy.at[0, y, :, other],
            dst_ref=wy_in.at[other if back else z],
            send_sem=wyz_s.at[d - 1],
            recv_sem=wyz_r.at[d - 1],
            device_id=dev(z_=other),
            device_id_type=MESH,
        )

    for i in range(3):
        scatter_block(4 + i)
        wz_ring.absorb(i)
        wy_ring.absorb(i)
    for d in range(1, z_n):
        wyz(d, False).start()
        pending.append(wyz(d, False).wait_send)
    scatter_block(7)
    wz_ring.absorb(3)
    for zb in range(z_n):
        to_pair(zb).wait_recv()
        cg[own_words(zb, x), :] += cg_x[zb]
    for i in range(2):
        cg_ring.send(i)
    for i in range(3):
        wz_ring.absorb(4 + i)
        cg_ring.absorb(i)
    for d in range(1, y_n):
        wzy(d, False).start()
        pending.append(wzy(d, False).wait_send)
    wy_in[z] = wy[0, y, :, z]
    wz_in[y] = wz[0, z, :, y]
    cg_ring.absorb(3)
    for d in range(1, z_n):
        wyz(d, True).wait_recv()
    acc = wy_in[0]
    for i in range(1, z_n):
        acc = acc + wy_in[i]
    total[:, :, :half_d] = acc
    for d in range(1, y_n):
        wzy(d, True).wait_recv()
    acc = wz_in[0]
    for i in range(1, y_n):
        acc = acc + wz_in[i]
    total[:, :, half_d:] = acc

    def last(k):
        xh_, x_ = turn(xh, k // 2, xh_n), turn(x, k % 2, x_n)
        return pltpu.make_async_remote_copy(
            src_ref=total.at[xh_],
            dst_ref=final.at[k - 1],
            send_sem=fin_s.at[k - 1],
            recv_sem=fin_r.at[k - 1],
            device_id=dev(dom_of(xh_, y, c), x_=x_),
            device_id_type=MESH,
        )

    for k in range(1, 4):
        last(k).start()
        pending.append(last(k).wait_send)
    for i in range(4, 7):
        cg_ring.absorb(i)
    cg_ref[...] = cg[own_words(z, x), :]
    acc = total[xh]
    for k in range(1, 4):
        last(k).wait_recv()
        acc = acc + final[k - 1]
    wg_ref[...] = jnp.where(x == 0, acc[:4], acc[4:])

    for wait in pending:
        wait()


def per_device(sizes, queries_in, encoder_weight, codebook, codes, positive_ids, loss_weight):
    xh_n, y_n, c_n, z_n, x_n = sizes
    q_rows, d_model = queries_in.shape[1:]
    w_rows = encoder_weight.shape[0]
    subs, width, words = codebook.shape[1:]
    n_pass, n_sub = codes.shape[1:]
    blk = w_rows * d_model // 128
    group, doms, half = z_n * x_n, xh_n * y_n * c_n, d_model // 2
    w = encoder_weight.reshape(w_rows, d_model // 128, 128).transpose(1, 0, 2).reshape(blk, 128)

    def ring_bufs(n, rows, lanes):
        return 2 * [
            pltpu.VMEM((2, n - 1, rows, lanes), jnp.int16),
            pltpu.VMEM((2, n - 1, 8, lanes), F32),
        ]

    vmem = pl.BlockSpec(memory_space=pltpu.VMEM)
    dma = pltpu.SemaphoreType.DMA
    wg, cg = pl.pallas_call(
        functools.partial(kernel, sizes),
        out_shape=(
            jax.ShapeDtypeStruct((w_rows, d_model), F32),
            jax.ShapeDtypeStruct((d_model // group, words), F32),
        ),
        in_specs=[vmem] * 6,
        out_specs=(vmem, vmem),
        scratch_shapes=[
            pltpu.VMEM((doms, group, blk, 128), BF16),
            pltpu.VMEM((d_model, d_model), BF16),
            pltpu.VMEM((2, d_model // 2, q_rows), BF16),
            pltpu.VMEM((z_n, subs * width, words), BF16),
            pltpu.VMEM((n_sub, n_pass), jnp.int32),
            pltpu.VMEM((d_model, n_pass), BF16),
            pltpu.VMEM((n_pass, d_model), BF16),
            pltpu.VMEM((z_n, d_model, q_rows), BF16),
            pltpu.VMEM((d_model, z_n * q_rows), BF16),
            pltpu.VMEM((z_n, n_pass, q_rows), F32),
            pltpu.VMEM((n_pass, z_n * q_rows), BF16),
            pltpu.VMEM((z_n, d_model, q_rows), F32),
            pltpu.VMEM((d_model, n_pass), F32),
            pltpu.VMEM((d_model, q_rows), F32),
            pltpu.VMEM((z_n, 8, 128), F32),
            pltpu.VMEM((d_model, q_rows), BF16),
            pltpu.VMEM((d_model, words), F32),
            pltpu.VMEM((z_n, d_model // group, words), F32),
            pltpu.VMEM((3, z_n, xh_n, y_n, 8, half), F32),
            pltpu.VMEM((3, y_n, xh_n, z_n, 8, half), F32),
            pltpu.VMEM((y_n, xh_n, 8, half), F32),
            pltpu.VMEM((z_n, xh_n, 8, half), F32),
            pltpu.VMEM((xh_n, 8, d_model), F32),
            pltpu.VMEM((3, 8, d_model), F32),
            *ring_bufs(z_n, half, q_rows),
            *ring_bufs(z_n, d_model // group // 2, words),
            *ring_bufs(z_n, y_n * 8, half),
            *ring_bufs(y_n, z_n * 8, half),
            dma((z_n - 1,)),
            dma((z_n - 1,)),
            dma((3,)),
            dma((3,)),
            dma((2, 2, y_n // 2)),
            dma((2, 2, y_n // 2)),
            dma((2, y_n)),
            dma((2, y_n)),
            dma((2, z_n // 2)),
            dma((2, z_n // 2)),
            dma((2, z_n - 1)),
            dma((2, z_n - 1)),
            dma((z_n - 1,)),
            dma((z_n - 1,)),
            dma((2, z_n - 1, 2)),
            dma((2, z_n - 1, 2)),
            dma((z_n,)),
            dma((z_n,)),
            dma((2, z_n - 1, 2)),
            dma((2, z_n - 1, 2)),
            dma((2,)),
            dma((2,)),
            dma((2, z_n - 1, 2)),
            dma((2, z_n - 1, 2)),
            dma((2, y_n - 1, 2)),
            dma((2, y_n - 1, 2)),
            dma((y_n - 1,)),
            dma((y_n - 1,)),
            dma((z_n - 1,)),
            dma((z_n - 1,)),
            dma((3,)),
            dma((3,)),
        ],
        compiler_params=pltpu.CompilerParams(
            collective_id=0, has_side_effects=True, vmem_limit_bytes=60 * 2**20
        ),
        name="encoder_codebook_grads",
    )(
        w,
        queries_in[0],
        codebook.reshape(subs * width, words),
        codes[0],
        positive_ids.reshape(group, q_rows),
        loss_weight.reshape(group, q_rows).astype(F32),
    )
    return wg, cg.reshape(1, n_sub // group, width, words)


def solution(mesh):
    doms = mesh.shape["dom"]
    sizes = (2, doms // 4, 2, mesh.shape["shard"], mesh.shape["dp"])
    return jax.shard_map(
        functools.partial(per_device, sizes),
        mesh=mesh,
        in_specs=(
            P("dom", ("shard", "dp"), None),
            P(("dom", "shard", "dp"), None),
            P("dom", "shard", None, None),
            P("dom", "shard", None),
            P("dom", None),
            P("dom", None),
        ),
        out_specs=(P(("dom", "shard", "dp"), None), P("dom", ("shard", "dp"), None, None)),
        check_vma=False,
    )
```

```python
import functools

import jax
import jax.numpy as jnp
from jax import lax
from jax.experimental import pallas as pl
from jax.experimental.pallas import tpu as pltpu
from jax.sharding import PartitionSpec as P

MESH = pl.DeviceIdType.MESH
BF16 = jnp.bfloat16
F32 = jnp.float32
EPS = 1e-06
NT = (((1,), (1,)), ((), ()))


class Ring:
    def __init__(self, slot, half, me, n, dev, send_sem, recv_sem):
        self.slot, self.half, self.me, self.n, self.dev = slot, half, me, n, dev
        self.send_sem, self.recv_sem, self.k = send_sem, recv_sem, n // 2

    def at(self, offset):
        return lax.rem(self.me + offset + self.n, self.n)

    def copies(self, s, shift):
        views = (self.slot, self.slot) if s < self.k - 1 else (lambda i: self.half(i, 0), lambda i: self.half(i, 1))
        out = []
        for way, sign in ((0, 1), (1, -1)):
            ref = views[way](self.at(-sign * (s + shift)))
            out.append(
                pltpu.make_async_remote_copy(
                    src_ref=ref,
                    dst_ref=ref,
                    send_sem=self.send_sem.at[way, s],
                    recv_sem=self.recv_sem.at[way, s],
                    device_id=self.dev(self.at(sign)),
                    device_id_type=MESH,
                )
            )
        return out

    def start(self, s):
        for copy in self.copies(s, 0):
            copy.start()

    def recv(self, s):
        for copy in self.copies(s, 1):
            copy.wait_recv()

    def finish(self):
        for s in range(self.k):
            for copy in self.copies(s, 0):
                copy.wait_send()


def quantize(value):
    largest = jnp.maximum(jnp.max(jnp.abs(value), axis=0, keepdims=True), 1e-30)
    whole = jnp.round(value * (32767.0 / largest)).astype(jnp.int32).astype(jnp.int16)
    return whole, largest * (1.0 / 32767.0)


def restore(whole, step):
    return whole.astype(jnp.int32).astype(F32) * step


class HalfRing:
    def __init__(self, half, me, n, right, left, send_sem, recv_sem):
        self.half, self.me, self.n, self.to = half, me, n, (right, left)
        self.send_sem, self.recv_sem = send_sem, recv_sem
        k = n // 2
        self.order = [(d, h) for d in range(k - 1) for h in (0, 1)] + [(k - 1, 0)]

    def copy(self, way, i, farther):
        d, h = self.order[i]
        d += farther
        ref = self.half(lax.rem(self.me + (d if way else self.n - d), self.n), 1 - h if way else h)
        return pltpu.make_async_remote_copy(
            src_ref=ref,
            dst_ref=ref,
            send_sem=self.send_sem.at[way, i],
            recv_sem=self.recv_sem.at[way, i],
            device_id=self.to[way],
            device_id_type=MESH,
        )

    def start(self, i):
        for way in range(2):
            self.copy(way, i, 0).start()

    def pass_on(self, i):
        for way in range(2):
            self.copy(way, i, 1).wait_recv()
            if i + 2 < len(self.order):
                self.copy(way, i + 2, 0).start()

    def finish(self):
        for i in range(len(self.order)):
            for way in range(2):
                self.copy(way, i, 0).wait_send()


class RingSum:
    def __init__(self, view, bufs, n, right, left, send_sem, recv_sem):
        self.view, self.n, self.to = view, n, (right, left)
        self.out, self.out_step, self.slots, self.steps = bufs
        self.send_sem, self.recv_sem = send_sem, recv_sem
        k = n // 2
        self.order = [(k, 0)] + [(j, h) for j in range(k - 1, 0, -1) for h in (1, 0)]
        self.rows, self.lanes = self.out.shape[2:]
        self.tall = self.rows == 512

    def part(self, way, i, nearer):
        j, h = self.order[i]
        j -= nearer
        return self.view((self.n - j) % self.n, 1 - h) if way else self.view(j, h)

    def copies(self, way, i):
        return [
            pltpu.make_async_remote_copy(
                src_ref=src.at[way, i],
                dst_ref=dst.at[way, i],
                send_sem=self.send_sem.at[way, i, t],
                recv_sem=self.recv_sem.at[way, i, t],
                device_id=self.to[way],
                device_id_type=MESH,
            )
            for t, (src, dst) in enumerate(((self.out, self.slots), (self.out_step, self.steps)))
        ]

    def groups(self):
        return [(g, slice(g * 64, (g + 1) * 64)) for g in range(8)] if self.tall else [(0, slice(0, self.rows))]

    def start(self, way, i):
        part = self.part(way, i, 0)
        steps = []
        for _, rows in self.groups():
            value = part[rows, :] if self.tall else part[...].reshape(self.rows, self.lanes)
            self.out[way, i, rows, :], step = quantize(value)
            steps.append(step)
        self.out_step[way, i] = jnp.concatenate(steps, 0) if self.tall else steps[0]
        for copy in self.copies(way, i):
            copy.start()

    def send(self, i):
        for way in range(2):
            self.start(way, i)

    def absorb(self, i):
        for way in range(2):
            for copy in self.copies(way, i):
                copy.wait_recv()
            part = self.part(way, i, 1)
            for g, rows in self.groups():
                value = restore(self.slots[way, i, rows, :], self.steps[way, i, g : g + 1, :])
                if self.tall:
                    part[rows, :] += value
                else:
                    part[...] += value.reshape(part.shape)
            if i + 2 < len(self.order):
                self.start(way, i + 2)

    def finish(self):
        for i in range(len(self.order)):
            for way in range(2):
                for copy in self.copies(way, i):
                    copy.wait_send()


def kernel(
    sizes,
    w_ref,
    x_ref,
    book_ref,
    codes_ref,
    pos_ref,
    wt_ref,
    wg_ref,
    cg_ref,
    g_all,
    w_full,
    xt,
    books,
    codes_t,
    pt,
    pas,
    qs,
    q_cat,
    exps,
    gs_cat,
    gn,
    gpt,
    normed_t,
    tots,
    ge_t,
    cg,
    cg_x,
    wz,
    wy,
    wzy_out,
    wzy_out_step,
    wzy_in,
    wzy_in_step,
    wyz_out,
    wyz_out_step,
    wyz_in,
    wyz_in_step,
    total,
    final,
    gn_out,
    gn_out_step,
    gn_in,
    gn_in_step,
    cg_out,
    cg_out_step,
    cg_in,
    cg_in_step,
    wz_out,
    wz_out_step,
    wz_got,
    wz_got_step,
    wy_out,
    wy_out_step,
    wy_got,
    wy_got_step,
    a1_s,
    a1_r,
    a2_s,
    a2_r,
    y_s,
    y_r,
    core_s,
    core_r,
    book_s,
    book_r,
    q_s,
    q_r,
    tot_s,
    tot_r,
    gn_s,
    gn_r,
    cx_s,
    cx_r,
    cz_s,
    cz_r,
    wc_s,
    wc_r,
    wz_s,
    wz_r,
    wy_s,
    wy_r,
    wzy_s,
    wzy_r,
    wyz_s,
    wyz_r,
    fin_s,
    fin_r,
):
    xh_n, y_n, c_n, z_n, x_n = sizes
    dom, z, x = lax.axis_index("dom"), lax.axis_index("shard"), lax.axis_index("dp")
    xh, y, c = dom // (y_n * c_n), lax.rem(dom // c_n, y_n), lax.rem(dom, c_n)

    def dom_of(xh_, y_, c_):
        return (xh_ * y_n + y_) * c_n + c_

    def dev(dom_=None, z_=None, x_=None):
        return {
            "dom": dom if dom_ is None else dom_,
            "shard": z if z_ is None else z_,
            "dp": x if x_ is None else x_,
        }

    def turn(i, d, n):
        return lax.rem(i + d + n, n)

    pending = []
    peers = [dev(z_=turn(z, dz, z_n)) for dz in range(1, z_n)] + [dev(x_=turn(x, 1, x_n))]
    peers += [dev(dom_of(turn(xh, 1, xh_n), y, c)), dev(dom_of(turn(xh, 1, xh_n), y, c), x_=turn(x, 1, x_n))]
    peers += [dev(dom_of(xh, turn(y, dy, y_n), c)) for dy in range(1, y_n)]
    peers += [dev(dom_of(xh, y, turn(c, 1, c_n)))]
    barrier = pltpu.get_barrier_semaphore()
    for peer in peers:
        pl.semaphore_signal(barrier, inc=1, device_id=peer, device_id_type=MESH)

    mine = x * z_n + z
    g_all[dom, mine] = w_ref[...]
    books[z] = book_ref[...].astype(BF16)
    pl.semaphore_wait(barrier, len(peers))

    def a1(d, back):
        z_ = turn(z, -d if back else d, z_n)
        ref = g_all.at[dom, x * z_n + z_ if back else mine]
        return pltpu.make_async_remote_copy(
            src_ref=ref,
            dst_ref=ref,
            send_sem=a1_s.at[d - 1],
            recv_sem=a1_r.at[d - 1],
            device_id=dev(z_=z_),
            device_id_type=MESH,
        )

    for d in range(1, z_n):
        a1(d, False).start()
        pending.append(a1(d, False).wait_send)
    book_ring = Ring(
        lambda i: books.at[i],
        lambda i, h: books.at[i, pl.ds(h * (books.shape[1] // 2), books.shape[1] // 2)],
        z,
        z_n,
        lambda i: dev(z_=i),
        book_s,
        book_r,
    )
    book_ring.start(0)
    pending.append(book_ring.finish)

    n_sub, n_pass = codes_t.shape
    for i in range(n_pass // 128):
        codes_t[:, i * 128 : (i + 1) * 128] = codes_ref[i * 128 : (i + 1) * 128, :].T
    for i in range(x_ref.shape[1] // 128):
        turned = x_ref[:, i * 128 : (i + 1) * 128].astype(F32).T.astype(BF16)
        for h in range(2):
            xt[h, i * 64 : (i + 1) * 64, :] = turned[h * 64 : (h + 1) * 64]

    xh2, x2 = turn(xh, 1, xh_n), turn(x, 1, x_n)

    def a2(k, back):
        dom_, x_ = dom_of(xh2 if k // 2 else xh, y, c), x2 if k % 2 else x
        ref = g_all.at[dom_ if back else dom, pl.ds((x_ if back else x) * z_n, z_n)]
        return pltpu.make_async_remote_copy(
            src_ref=ref,
            dst_ref=ref,
            send_sem=a2_s.at[k - 1],
            recv_sem=a2_r.at[k - 1],
            device_id=dev(dom_, x_=x_),
            device_id_type=MESH,
        )

    for d in range(1, z_n):
        a1(d, True).wait_recv()
    for k in range(1, 4):
        a2(k, False).start()
        pending.append(a2(k, False).wait_send)

    def y_ring(j, xh_):
        half = g_all.shape[1] // 2
        return Ring(
            lambda i: g_all.at[dom_of(xh_, i, c)],
            lambda i, h: g_all.at[dom_of(xh_, i, c), pl.ds(h * half, half)],
            y,
            y_n,
            lambda i: dev(dom_of(xh, i, c)),
            y_s.at[j],
            y_r.at[j],
        )

    def core(j, dy, back):
        ref = g_all.at[dom_of(xh2 if j else xh, turn(y, dy, y_n), turn(c, 1, c_n) if back else c)]
        return pltpu.make_async_remote_copy(
            src_ref=ref,
            dst_ref=ref,
            send_sem=core_s.at[j, dy],
            recv_sem=core_r.at[j, dy],
            device_id=dev(dom_of(xh, y, turn(c, 1, c_n))),
            device_id_type=MESH,
        )

    blk, col_blocks = w_ref.shape[0], x_ref.shape[1] // 128
    r_rows = blk // col_blocks
    per = 16 // r_rows
    rows = blk * per
    o = lax.broadcasted_iota(jnp.int32, (rows, rows), 0)
    j_ = lax.broadcasted_iota(jnp.int32, (rows, rows), 1)
    perm = (
        (j_ == (lax.rem(o, 16) // r_rows) * blk + (o // 16) * r_rows + lax.rem(o, r_rows)).astype(F32).astype(BF16)
    )

    def assemble(dom_):
        for t in range(g_all.shape[1] // per):
            blocks = [g_all[dom_, (b % x_n) * z_n + b // x_n] for b in range(t * per, (t + 1) * per)]
            part = jnp.dot(perm, jnp.concatenate(blocks, 0), preferred_element_type=F32).astype(BF16)
            row = pl.multiple_of((dom_ * (g_all.shape[1] // per) + t) * 16, 16)
            for cb in range(col_blocks):
                w_full[pl.ds(row, 16), cb * 128 : (cb + 1) * 128] = part[cb * 16 : (cb + 1) * 16]

    def rebuild(zb):
        groups = books.shape[1] // 64

        def per_group(gi, carry):
            r = pl.multiple_of(gi * 64, 64)
            table = books[zb, pl.ds(r, 64), :].astype(F32)
            out_row = pl.multiple_of(zb * books.shape[1] + r, 64)
            code_row = pl.multiple_of((zb * groups + gi) * 8, 8)

            def per_block(i, inner):
                for u in range(2):
                    p0 = pl.multiple_of(i * 256 + u * 128, 128)
                    cc = codes_t[pl.ds(code_row, 8), pl.ds(p0, 128)]
                    for jj in range(4):
                        parts = []
                        for j in (2 * jj, 2 * jj + 1):
                            idx = jnp.broadcast_to(cc[j : j + 1, :], (8, 128))
                            low = idx & 127
                            lo = jnp.take_along_axis(
                                table[j * 8 : j * 8 + 8, :128], low, axis=1, mode="promise_in_bounds"
                            )
                            hi = jnp.take_along_axis(
                                table[j * 8 : j * 8 + 8, 128:], low, axis=1, mode="promise_in_bounds"
                            )
                            parts.append(jnp.where(idx >= 128, hi, lo))
                        pt[pl.ds(pl.multiple_of(out_row + jj * 16, 16), 16), pl.ds(p0, 128)] = jnp.concatenate(
                            parts, 0
                        ).astype(BF16)
                return inner

            return lax.fori_loop(0, n_pass // 256, per_block, carry)

        lax.fori_loop(0, groups, per_group, 0)

    ring0, ring1 = y_ring(0, xh), y_ring(1, xh2)
    pending += [ring0.finish, ring1.finish]
    pending += [core(j, dy, False).wait_send for j in range(2) for dy in range(y_n)]
    a2(1, True).wait_recv()
    ring0.start(0)
    core(0, 0, False).start()
    a2(2, True).wait_recv()
    a2(3, True).wait_recv()
    ring1.start(0)
    core(1, 0, False).start()
    rebuild(z)
    book_ring.recv(0)
    book_ring.start(1)
    rebuild(turn(z, 1, z_n))
    ring0.recv(0)
    ring0.start(1)
    core(0, 1, False).start()
    core(0, 3, False).start()
    rebuild(turn(z, -1, z_n))
    book_ring.recv(1)
    book_ring.start(2)
    ring1.recv(0)
    ring1.start(1)
    core(1, 1, False).start()
    core(1, 3, False).start()
    assemble(dom_of(xh, y, c))
    assemble(dom_of(xh2, y, c))
    ring0.recv(1)
    core(0, 2, False).start()
    book_ring.recv(2)
    book_ring.start(3)
    for dy in (1, 3):
        assemble(dom_of(xh, turn(y, dy, y_n), c))
        assemble(dom_of(xh2, turn(y, dy, y_n), c))
    ring1.recv(1)
    core(1, 2, False).start()
    for j in range(2):
        assemble(dom_of(xh2 if j else xh, turn(y, 2, y_n), c))
    for dy in (0, 1, 3, 2):
        for j in range(2):
            core(j, dy, True).wait_recv()
            assemble(dom_of(xh2 if j else xh, turn(y, dy, y_n), turn(c, 1, c_n)))

    d_model = x_ref.shape[1]
    squares = jnp.zeros((1, 128), F32)
    for i in range(d_model // 256):
        enc = jnp.dot(x_ref[...], w_full[:, i * 256 : (i + 1) * 256], preferred_element_type=F32)
        for h in range(2):
            enc_t = enc[:, h * 128 : (h + 1) * 128].T
            squares = squares + jnp.sum(enc_t * enc_t, axis=0, keepdims=True)
            normed_t[i * 256 + h * 128 : i * 256 + (h + 1) * 128, :] = enc_t
    inv_rms = lax.rsqrt(squares / d_model + EPS)
    for i in range(d_model // 128):
        value = normed_t[i * 128 : (i + 1) * 128, :] * inv_rms
        normed_t[i * 128 : (i + 1) * 128, :] = value
        qs[z, i * 128 : (i + 1) * 128, :] = value.astype(BF16)

    half_d = d_model // 2
    right, left = dev(z_=turn(z, 1, z_n)), dev(z_=turn(z, -1, z_n))
    q_ring = HalfRing(lambda i, h: qs.at[i, pl.ds(h * half_d, half_d)], z, z_n, right, left, q_s, q_r)
    q_ring.start(0)
    q_ring.start(1)
    pending.append(q_ring.finish)
    rebuild(turn(z, 2, z_n))
    rebuild(turn(z, -2, z_n))
    q_ring.pass_on(0)
    rebuild(turn(z, 3, z_n))
    rebuild(turn(z, -3, z_n))
    q_ring.pass_on(1)
    book_ring.recv(3)
    rebuild(turn(z, 4, z_n))
    q_ring.pass_on(2)

    def flip(i, carry):
        f0 = pl.multiple_of(i * 128, 128)
        for t in range(n_pass // 128):
            pas[t * 128 : (t + 1) * 128, pl.ds(f0, 128)] = (
                pt[pl.ds(f0, 128), t * 128 : (t + 1) * 128].astype(F32).T.astype(BF16)
            )
        return carry

    lax.fori_loop(0, d_model // 128, flip, 0)

    sub8 = lax.broadcasted_iota(jnp.int32, (8, 128), 0)

    def score(j, totals):
        b = turn(z, j, z_n)
        block = qs[b]
        q_cat[:, j * 128 : (j + 1) * 128] = block
        total = jnp.zeros((1, 128), F32)
        for t in range(n_pass // 256):
            s = jnp.dot(pas[t * 256 : (t + 1) * 256, :], block, preferred_element_type=F32)
            e = jnp.exp(s)
            exps[j, t * 256 : (t + 1) * 256, :] = e
            total = total + jnp.sum(e, axis=0, keepdims=True)
        return totals + jnp.where(sub8 == b, jnp.broadcast_to(total, (8, 128)), 0.0)

    totals = score(0, jnp.zeros((8, 128), F32))
    q_ring.pass_on(3)
    totals = score(1, totals)
    totals = score(7, totals)
    q_ring.pass_on(4)
    totals = score(2, totals)
    totals = score(6, totals)
    q_ring.pass_on(5)
    totals = score(3, totals)
    totals = score(5, totals)
    q_ring.pass_on(6)
    totals = score(4, totals)

    tots[z] = totals

    def tot(d, back):
        other = turn(z, -d if back else d, z_n)
        ref = tots.at[other if back else z]
        return pltpu.make_async_remote_copy(
            src_ref=ref,
            dst_ref=ref,
            send_sem=tot_s.at[d - 1],
            recv_sem=tot_r.at[d - 1],
            device_id=dev(z_=other),
            device_id_type=MESH,
        )

    for d in range(1, z_n):
        tot(d, False).start()
        pending.append(tot(d, False).wait_send)
    for d in range(1, z_n):
        tot(d, True).wait_recv()
    totals = tots[0]
    for i in range(1, z_n):
        totals = totals + tots[i]
    inverse = 1.0 / totals

    sub16 = lax.broadcasted_iota(jnp.int32, (16, 128), 0)
    first = z * n_pass
    weights_all, pos_all = wt_ref[...], pos_ref[...]

    def grads(j):
        b = turn(z, j, z_n)
        inv = jnp.sum(jnp.where(sub8 == b, inverse, 0.0), axis=0, keepdims=True)
        wt = jnp.sum(jnp.where(sub16 == b * x_n + x, weights_all, 0.0), axis=0, keepdims=True)
        pos = jnp.sum(jnp.where(sub16 == b * x_n + x, pos_all, 0), axis=0, keepdims=True) - first
        for t in range(n_pass // 256):
            e = exps[j, t * 256 : (t + 1) * 256, :]
            ids = lax.broadcasted_iota(jnp.int32, (256, 128), 0) + t * 256
            prob = e * inv
            gs_cat[t * 256 : (t + 1) * 256, j * 128 : (j + 1) * 128] = (
                wt * jnp.where(ids == pos, prob - 1.0, prob)
            ).astype(BF16)
        block = gs_cat[:, j * 128 : (j + 1) * 128]
        for t in range(d_model // 256):
            gn[j, t * 256 : (t + 1) * 256, :] = jnp.dot(
                pt[t * 256 : (t + 1) * 256, :], block, preferred_element_type=F32
            )

    gn_ring = RingSum(
        lambda j, h: gn.at[j, pl.ds(h * half_d, half_d)], (gn_out, gn_out_step, gn_in, gn_in_step), z_n, right, left, gn_s, gn_r
    )
    pending.append(gn_ring.finish)
    grads(4)
    gn_ring.send(0)
    grads(3)
    grads(5)
    gn_ring.send(1)
    gn_ring.absorb(0)
    grads(2)
    grads(6)
    gn_ring.absorb(1)
    grads(1)
    grads(7)
    grads(0)

    def passage_grads(i, carry):
        p0 = pl.multiple_of(i * 256, 256)
        gpt[:, pl.ds(p0, 256)] = lax.dot_general(
            q_cat[...], gs_cat[pl.ds(p0, 256), :], NT, preferred_element_type=F32
        )
        return carry

    lax.fori_loop(0, n_pass // 256, passage_grads, 0)

    gn_ring.absorb(2)

    levels = lax.broadcasted_iota(jnp.int32, (64, n_pass), 0).astype(BF16)

    def scatter(lo_m, hi_m):
        def per_subs(i, carry):
            for u in range(4):
                m = i * 4 + u
                r = pl.multiple_of(m * 8, 8)
                code = codes_t[pl.ds(m, 1), :]
                low = (code & 63).astype(BF16)
                high = jnp.broadcast_to(lax.shift_right_logical(code, 6).astype(BF16), (16, n_pass))
                g = gpt[pl.ds(r, 8), :]
                g_hi = g.astype(BF16).astype(F32)
                g16 = jnp.concatenate([g_hi, g - g_hi], 0).astype(BF16)
                left = jnp.concatenate([jnp.where(high == BF16(h), g16, BF16(0)) for h in range(4)], 0)
                onehot = jnp.where(levels == jnp.broadcast_to(low, (64, n_pass)), BF16(1), BF16(0))
                out = lax.dot_general(left, onehot, NT, preferred_element_type=F32)
                cg[pl.ds(r, 8), :] = jnp.concatenate(
                    [out[h * 16 : h * 16 + 8] + out[h * 16 + 8 : h * 16 + 16] for h in range(4)], 1
                )
            return carry

        lax.fori_loop(lo_m // 4, hi_m // 4, per_subs, 0)

    own_rows = cg.shape[0] // (z_n * x_n)

    def own_words(zb, dp):
        return pl.ds(pl.multiple_of((zb * x_n + dp) * own_rows, own_rows), own_rows)

    def to_pair(zb):
        return pltpu.make_async_remote_copy(
            src_ref=cg.at[own_words(zb, turn(x, 1, x_n))],
            dst_ref=cg_x.at[zb],
            send_sem=cx_s.at[zb],
            recv_sem=cx_r.at[zb],
            device_id=dev(x_=turn(x, 1, x_n)),
            device_id_type=MESH,
        )

    def scatter_block(zb):
        scatter(zb * n_sub // z_n, (zb + 1) * n_sub // z_n)
        to_pair(zb).start()
        pending.append(to_pair(zb).wait_send)

    for zb in range(4):
        scatter_block(zb)
        gn_ring.absorb(zb + 3)

    inner = jnp.zeros((1, 128), F32)
    for i in range(d_model // 256):
        part = slice(i * 256, (i + 1) * 256)
        inner = inner + jnp.sum(gn[0, part, :] * normed_t[part, :], axis=0, keepdims=True)
    inner = inner / d_model
    for i in range(d_model // 256):
        part = slice(i * 256, (i + 1) * 256)
        ge_t[part, :] = (inv_rms * (gn[0, part, :] - normed_t[part, :] * inner)).astype(BF16)

    def share(i, core_, right_half):
        out = lax.dot_general(
            xt[core_], ge_t[half_d:, :] if right_half else ge_t[:half_d, :], NT, preferred_element_type=F32
        )
        for xh_ in range(xh_n):
            for y_ in range(y_n):
                for z_ in range(z_n):
                    tile = out[((xh_ * y_n + y_) * z_n + z_) * 8 : ((xh_ * y_n + y_) * z_n + z_) * 8 + 8]
                    if right_half:
                        wz[i, z_, xh_, y_] = tile
                    else:
                        wy[i, y_, xh_, z_] = tile

    sibling = turn(c, 1, c_n)

    def to_core(i):
        buf = (wz, wy)[i]
        return pltpu.make_async_remote_copy(
            src_ref=buf.at[1],
            dst_ref=buf.at[2],
            send_sem=wc_s.at[i],
            recv_sem=wc_r.at[i],
            device_id=dev(dom_of(xh, y, sibling)),
            device_id_type=MESH,
        )

    share(1, sibling, True)
    to_core(0).start()
    share(1, sibling, False)
    to_core(1).start()
    share(0, c, True)
    share(0, c, False)
    pending += [to_core(0).wait_send, to_core(1).wait_send]

    wz_ring = RingSum(
        lambda j, h: wz.at[0, turn(z, j, z_n), h], (wz_out, wz_out_step, wz_got, wz_got_step), z_n, right, left, wz_s, wz_r
    )
    wy_ring = RingSum(
        lambda j, h: wy.at[0, turn(y, j, y_n), h],
        (wy_out, wy_out_step, wy_got, wy_got_step),
        y_n,
        dev(dom_of(xh, turn(y, 1, y_n), c)),
        dev(dom_of(xh, turn(y, -1, y_n), c)),
        wy_s,
        wy_r,
    )

    def cg_half(j, h):
        row = (turn(z, j, z_n) * x_n + x) * own_rows + h * (own_rows // 2)
        return cg.at[pl.ds(pl.multiple_of(row, own_rows // 2), own_rows // 2)]

    cg_ring = RingSum(cg_half, (cg_out, cg_out_step, cg_in, cg_in_step), z_n, right, left, cz_s, cz_r)
    pending += [wz_ring.finish, wy_ring.finish, cg_ring.finish]

    to_core(0).wait_recv()
    for i in range(z_n):
        wz[0, i] += wz[2, i]
    for i in range(2):
        wz_ring.send(i)
    to_core(1).wait_recv()
    for i in range(y_n):
        wy[0, i] += wy[2, i]
    for i in range(2):
        wy_ring.send(i)
    def direct(bufs, send_sem, recv_sem, d, target):
        out, out_step, got, got_step = bufs
        return [
            pltpu.make_async_remote_copy(
                src_ref=src.at[d - 1],
                dst_ref=dst.at[d - 1],
                send_sem=send_sem.at[d - 1, t],
                recv_sem=recv_sem.at[d - 1, t],
                device_id=target,
                device_id_type=MESH,
            )
            for t, (src, dst) in enumerate(((out, got), (out_step, got_step)))
        ]

    wzy_bufs = (wzy_out, wzy_out_step, wzy_in, wzy_in_step)
    wyz_bufs = (wyz_out, wyz_out_step, wyz_in, wyz_in_step)

    def wzy(d):
        return direct(wzy_bufs, wzy_s, wzy_r, d, dev(dom_of(xh, turn(y, d, y_n), c)))

    def wyz(d):
        return direct(wyz_bufs, wyz_s, wyz_r, d, dev(z_=turn(z, d, z_n)))

    def spread(view, bufs, copies, n):
        for d in range(1, n):
            bufs[0][d - 1], bufs[1][d - 1] = quantize(view(d).reshape(xh_n * 8, half_d))
            for copy in copies(d):
                copy.start()
                pending.append(copy.wait_send)

    def collect(view, bufs, copies, n):
        acc = view(0).reshape(xh_n * 8, half_d)
        for d in range(1, n):
            for copy in copies(d):
                copy.wait_recv()
            acc = acc + restore(bufs[2][d - 1], bufs[3][d - 1])
        return acc.reshape(xh_n, 8, half_d)

    def wz_part(d):
        return wz[0, z, :, turn(y, d, y_n)]

    def wy_part(d):
        return wy[0, y, :, turn(z, d, z_n)]

    for i in range(3):
        scatter_block(4 + i)
        wz_ring.absorb(i)
        wy_ring.absorb(i)
    spread(wy_part, wyz_bufs, wyz, z_n)
    scatter_block(7)
    wz_ring.absorb(3)
    for zb in range(z_n):
        to_pair(zb).wait_recv()
        cg[own_words(zb, x), :] += cg_x[zb]
    for i in range(2):
        cg_ring.send(i)
    for i in range(3):
        wz_ring.absorb(4 + i)
        cg_ring.absorb(i)
    spread(wz_part, wzy_bufs, wzy, y_n)
    cg_ring.absorb(3)
    total[:, :, :half_d] = collect(wy_part, wyz_bufs, wyz, z_n)
    total[:, :, half_d:] = collect(wz_part, wzy_bufs, wzy, y_n)

    def last(k):
        xh_, x_ = turn(xh, k // 2, xh_n), turn(x, k % 2, x_n)
        return pltpu.make_async_remote_copy(
            src_ref=total.at[xh_],
            dst_ref=final.at[k - 1],
            send_sem=fin_s.at[k - 1],
            recv_sem=fin_r.at[k - 1],
            device_id=dev(dom_of(xh_, y, c), x_=x_),
            device_id_type=MESH,
        )

    for k in range(1, 4):
        last(k).start()
        pending.append(last(k).wait_send)
    for i in range(4, 7):
        cg_ring.absorb(i)
    cg_ref[...] = cg[own_words(z, x), :]
    acc = total[xh]
    for k in range(1, 4):
        last(k).wait_recv()
        acc = acc + final[k - 1]
    wg_ref[...] = jnp.where(x == 0, acc[:4], acc[4:])

    for wait in pending:
        wait()


def per_device(sizes, queries_in, encoder_weight, codebook, codes, positive_ids, loss_weight):
    xh_n, y_n, c_n, z_n, x_n = sizes
    q_rows, d_model = queries_in.shape[1:]
    w_rows = encoder_weight.shape[0]
    subs, width, words = codebook.shape[1:]
    n_pass, n_sub = codes.shape[1:]
    blk = w_rows * d_model // 128
    group, doms, half = z_n * x_n, xh_n * y_n * c_n, d_model // 2
    w = encoder_weight.reshape(w_rows, d_model // 128, 128).transpose(1, 0, 2).reshape(blk, 128)

    def ring_bufs(n, rows, lanes):
        return 2 * [
            pltpu.VMEM((2, n - 1, rows, lanes), jnp.int16),
            pltpu.VMEM((2, n - 1, 8 if rows == 512 else 1, lanes), F32),
        ]

    def direct_bufs(n, rows, lanes):
        return 2 * [pltpu.VMEM((n - 1, rows, lanes), jnp.int16), pltpu.VMEM((n - 1, 1, lanes), F32)]

    vmem = pl.BlockSpec(memory_space=pltpu.VMEM)
    dma = pltpu.SemaphoreType.DMA
    wg, cg = pl.pallas_call(
        functools.partial(kernel, sizes),
        out_shape=(
            jax.ShapeDtypeStruct((w_rows, d_model), F32),
            jax.ShapeDtypeStruct((d_model // group, words), F32),
        ),
        in_specs=[vmem] * 6,
        out_specs=(vmem, vmem),
        scratch_shapes=[
            pltpu.VMEM((doms, group, blk, 128), BF16),
            pltpu.VMEM((d_model, d_model), BF16),
            pltpu.VMEM((2, d_model // 2, q_rows), BF16),
            pltpu.VMEM((z_n, subs * width, words), BF16),
            pltpu.VMEM((n_sub, n_pass), jnp.int32),
            pltpu.VMEM((d_model, n_pass), BF16),
            pltpu.VMEM((n_pass, d_model), BF16),
            pltpu.VMEM((z_n, d_model, q_rows), BF16),
            pltpu.VMEM((d_model, z_n * q_rows), BF16),
            pltpu.VMEM((z_n, n_pass, q_rows), F32),
            pltpu.VMEM((n_pass, z_n * q_rows), BF16),
            pltpu.VMEM((z_n, d_model, q_rows), F32),
            pltpu.VMEM((d_model, n_pass), F32),
            pltpu.VMEM((d_model, q_rows), F32),
            pltpu.VMEM((z_n, 8, 128), F32),
            pltpu.VMEM((d_model, q_rows), BF16),
            pltpu.VMEM((d_model, words), F32),
            pltpu.VMEM((z_n, d_model // group, words), F32),
            pltpu.VMEM((3, z_n, xh_n, y_n, 8, half), F32),
            pltpu.VMEM((3, y_n, xh_n, z_n, 8, half), F32),
            *direct_bufs(y_n, xh_n * 8, half),
            *direct_bufs(z_n, xh_n * 8, half),
            pltpu.VMEM((xh_n, 8, d_model), F32),
            pltpu.VMEM((3, 8, d_model), F32),
            *ring_bufs(z_n, half, q_rows),
            *ring_bufs(z_n, d_model // group // 2, words),
            *ring_bufs(z_n, y_n * 8, half),
            *ring_bufs(y_n, z_n * 8, half),
            dma((z_n - 1,)),
            dma((z_n - 1,)),
            dma((3,)),
            dma((3,)),
            dma((2, 2, y_n // 2)),
            dma((2, 2, y_n // 2)),
            dma((2, y_n)),
            dma((2, y_n)),
            dma((2, z_n // 2)),
            dma((2, z_n // 2)),
            dma((2, z_n - 1)),
            dma((2, z_n - 1)),
            dma((z_n - 1,)),
            dma((z_n - 1,)),
            dma((2, z_n - 1, 2)),
            dma((2, z_n - 1, 2)),
            dma((z_n,)),
            dma((z_n,)),
            dma((2, z_n - 1, 2)),
            dma((2, z_n - 1, 2)),
            dma((2,)),
            dma((2,)),
            dma((2, z_n - 1, 2)),
            dma((2, z_n - 1, 2)),
            dma((2, y_n - 1, 2)),
            dma((2, y_n - 1, 2)),
            dma((y_n - 1, 2)),
            dma((y_n - 1, 2)),
            dma((z_n - 1, 2)),
            dma((z_n - 1, 2)),
            dma((3,)),
            dma((3,)),
        ],
        compiler_params=pltpu.CompilerParams(
            collective_id=0, has_side_effects=True, vmem_limit_bytes=60 * 2**20
        ),
        name="encoder_codebook_grads",
    )(
        w,
        queries_in[0],
        codebook.reshape(subs * width, words),
        codes[0],
        positive_ids.reshape(group, q_rows),
        loss_weight.reshape(group, q_rows).astype(F32),
    )
    return wg, cg.reshape(1, n_sub // group, width, words)


def solution(mesh):
    doms = mesh.shape["dom"]
    sizes = (2, doms // 4, 2, mesh.shape["shard"], mesh.shape["dp"])
    return jax.shard_map(
        functools.partial(per_device, sizes),
        mesh=mesh,
        in_specs=(
            P("dom", ("shard", "dp"), None),
            P(("dom", "shard", "dp"), None),
            P("dom", "shard", None, None),
            P("dom", "shard", None),
            P("dom", None),
            P("dom", None),
        ),
        out_specs=(P(("dom", "shard", "dp"), None), P("dom", ("shard", "dp"), None, None)),
        check_vma=False,
    )
```

```python
import functools

import jax
import jax.numpy as jnp
from jax import lax
from jax.experimental import pallas as pl
from jax.experimental.pallas import tpu as pltpu
from jax.sharding import PartitionSpec as P

MESH = pl.DeviceIdType.MESH
BF16 = jnp.bfloat16
F32 = jnp.float32
EPS = 1e-06
NT = (((1,), (1,)), ((), ()))


class Ring:
    def __init__(self, slot, half, me, n, dev, send_sem, recv_sem):
        self.slot, self.half, self.me, self.n, self.dev = slot, half, me, n, dev
        self.send_sem, self.recv_sem, self.k = send_sem, recv_sem, n // 2

    def at(self, offset):
        return lax.rem(self.me + offset + self.n, self.n)

    def copies(self, s, shift):
        views = (self.slot, self.slot) if s < self.k - 1 else (lambda i: self.half(i, 0), lambda i: self.half(i, 1))
        out = []
        for way, sign in ((0, 1), (1, -1)):
            ref = views[way](self.at(-sign * (s + shift)))
            out.append(
                pltpu.make_async_remote_copy(
                    src_ref=ref,
                    dst_ref=ref,
                    send_sem=self.send_sem.at[way, s],
                    recv_sem=self.recv_sem.at[way, s],
                    device_id=self.dev(self.at(sign)),
                    device_id_type=MESH,
                )
            )
        return out

    def start(self, s):
        for copy in self.copies(s, 0):
            copy.start()

    def recv(self, s):
        for copy in self.copies(s, 1):
            copy.wait_recv()

    def finish(self):
        for s in range(self.k):
            for copy in self.copies(s, 0):
                copy.wait_send()


def quantize(value):
    largest = jnp.maximum(jnp.max(jnp.abs(value), axis=0, keepdims=True), 1e-30)
    whole = jnp.round(value * (32767.0 / largest)).astype(jnp.int32).astype(jnp.int16)
    return whole, largest * (1.0 / 32767.0)


def restore(whole, step):
    return whole.astype(jnp.int32).astype(F32) * step


class HalfRing:
    def __init__(self, half, me, n, right, left, send_sem, recv_sem):
        self.half, self.me, self.n, self.to = half, me, n, (right, left)
        self.send_sem, self.recv_sem = send_sem, recv_sem
        k = n // 2
        self.order = [(d, h) for d in range(k - 1) for h in (0, 1)] + [(k - 1, 0)]

    def copy(self, way, i, farther):
        d, h = self.order[i]
        d += farther
        ref = self.half(lax.rem(self.me + (d if way else self.n - d), self.n), 1 - h if way else h)
        return pltpu.make_async_remote_copy(
            src_ref=ref,
            dst_ref=ref,
            send_sem=self.send_sem.at[way, i],
            recv_sem=self.recv_sem.at[way, i],
            device_id=self.to[way],
            device_id_type=MESH,
        )

    def start(self, i):
        for way in range(2):
            self.copy(way, i, 0).start()

    def pass_on(self, i):
        for way in range(2):
            self.copy(way, i, 1).wait_recv()
            if i + 2 < len(self.order):
                self.copy(way, i + 2, 0).start()

    def finish(self):
        for i in range(len(self.order)):
            for way in range(2):
                self.copy(way, i, 0).wait_send()


class RingSum:
    def __init__(self, view, bufs, n, right, left, send_sem, recv_sem):
        self.view, self.n, self.to = view, n, (right, left)
        self.out, self.out_step, self.slots, self.steps = bufs
        self.send_sem, self.recv_sem = send_sem, recv_sem
        k = n // 2
        self.order = [(k, 0)] + [(j, h) for j in range(k - 1, 0, -1) for h in (1, 0)]
        self.rows, self.lanes = self.out.shape[2:]
        self.tall = self.rows == 512

    def part(self, way, i, nearer):
        j, h = self.order[i]
        j -= nearer
        return self.view((self.n - j) % self.n, 1 - h) if way else self.view(j, h)

    def copies(self, way, i):
        return [
            pltpu.make_async_remote_copy(
                src_ref=src.at[way, i],
                dst_ref=dst.at[way, i],
                send_sem=self.send_sem.at[way, i, t],
                recv_sem=self.recv_sem.at[way, i, t],
                device_id=self.to[way],
                device_id_type=MESH,
            )
            for t, (src, dst) in enumerate(((self.out, self.slots), (self.out_step, self.steps)))
        ]

    def groups(self):
        return [(g, slice(g * 64, (g + 1) * 64)) for g in range(8)] if self.tall else [(0, slice(0, self.rows))]

    def start(self, way, i):
        part = self.part(way, i, 0)
        steps = []
        for _, rows in self.groups():
            value = part[rows, :] if self.tall else part[...].reshape(self.rows, self.lanes)
            self.out[way, i, rows, :], step = quantize(value)
            steps.append(step)
        self.out_step[way, i] = jnp.concatenate(steps, 0) if self.tall else steps[0]
        for copy in self.copies(way, i):
            copy.start()

    def send(self, i):
        for way in range(2):
            self.start(way, i)

    def absorb(self, i):
        for way in range(2):
            for copy in self.copies(way, i):
                copy.wait_recv()
            part = self.part(way, i, 1)
            for g, rows in self.groups():
                value = restore(self.slots[way, i, rows, :], self.steps[way, i, g : g + 1, :])
                if self.tall:
                    part[rows, :] += value
                else:
                    part[...] += value.reshape(part.shape)
            if i + 2 < len(self.order):
                self.start(way, i + 2)

    def finish(self):
        for i in range(len(self.order)):
            for way in range(2):
                for copy in self.copies(way, i):
                    copy.wait_send()


def kernel(
    sizes,
    w_ref,
    x_ref,
    book_ref,
    codes_ref,
    pos_ref,
    wt_ref,
    wg_ref,
    cg_ref,
    g_all,
    w_full,
    xt,
    books,
    codes_t,
    pt,
    pas,
    qs,
    q_cat,
    exps,
    gs_cat,
    gn,
    gpt,
    normed_t,
    tots,
    ge_t,
    cg,
    cg_x,
    wz,
    wy,
    wzy_out,
    wzy_out_step,
    wzy_in,
    wzy_in_step,
    wyz_out,
    wyz_out_step,
    wyz_in,
    wyz_in_step,
    total,
    final,
    gn_out,
    gn_out_step,
    gn_in,
    gn_in_step,
    cg_out,
    cg_out_step,
    cg_in,
    cg_in_step,
    wz_out,
    wz_out_step,
    wz_got,
    wz_got_step,
    wy_out,
    wy_out_step,
    wy_got,
    wy_got_step,
    a1_s,
    a1_r,
    a2_s,
    a2_r,
    y_s,
    y_r,
    core_s,
    core_r,
    book_s,
    book_r,
    q_s,
    q_r,
    tot_s,
    tot_r,
    gn_s,
    gn_r,
    cx_s,
    cx_r,
    cz_s,
    cz_r,
    wc_s,
    wc_r,
    wz_s,
    wz_r,
    wy_s,
    wy_r,
    wzy_s,
    wzy_r,
    wyz_s,
    wyz_r,
    fin_s,
    fin_r,
):
    xh_n, y_n, c_n, z_n, x_n = sizes
    dom, z, x = lax.axis_index("dom"), lax.axis_index("shard"), lax.axis_index("dp")
    xh, y, c = dom // (y_n * c_n), lax.rem(dom // c_n, y_n), lax.rem(dom, c_n)

    def dom_of(xh_, y_, c_):
        return (xh_ * y_n + y_) * c_n + c_

    def dev(dom_=None, z_=None, x_=None):
        return {
            "dom": dom if dom_ is None else dom_,
            "shard": z if z_ is None else z_,
            "dp": x if x_ is None else x_,
        }

    def turn(i, d, n):
        return lax.rem(i + d + n, n)

    pending = []
    peers = [dev(z_=turn(z, dz, z_n)) for dz in range(1, z_n)] + [dev(x_=turn(x, 1, x_n))]
    peers += [dev(dom_of(turn(xh, 1, xh_n), y, c)), dev(dom_of(turn(xh, 1, xh_n), y, c), x_=turn(x, 1, x_n))]
    peers += [dev(dom_of(xh, turn(y, dy, y_n), c)) for dy in range(1, y_n)]
    peers += [dev(dom_of(xh, y, turn(c, 1, c_n)))]
    barrier = pltpu.get_barrier_semaphore()
    for peer in peers:
        pl.semaphore_signal(barrier, inc=1, device_id=peer, device_id_type=MESH)

    mine = x * z_n + z
    g_all[dom, mine] = w_ref[...]
    books[z] = book_ref[...].astype(BF16)
    pl.semaphore_wait(barrier, len(peers))

    def a1(d, back):
        z_ = turn(z, -d if back else d, z_n)
        ref = g_all.at[dom, x * z_n + z_ if back else mine]
        return pltpu.make_async_remote_copy(
            src_ref=ref,
            dst_ref=ref,
            send_sem=a1_s.at[d - 1],
            recv_sem=a1_r.at[d - 1],
            device_id=dev(z_=z_),
            device_id_type=MESH,
        )

    for d in range(1, z_n):
        a1(d, False).start()
        pending.append(a1(d, False).wait_send)
    book_ring = Ring(
        lambda i: books.at[i],
        lambda i, h: books.at[i, pl.ds(h * (books.shape[1] // 2), books.shape[1] // 2)],
        z,
        z_n,
        lambda i: dev(z_=i),
        book_s,
        book_r,
    )
    book_ring.start(0)
    pending.append(book_ring.finish)

    n_sub, n_pass = codes_t.shape
    for i in range(n_pass // 128):
        codes_t[:, i * 128 : (i + 1) * 128] = codes_ref[i * 128 : (i + 1) * 128, :].T
    for i in range(x_ref.shape[1] // 128):
        turned = x_ref[:, i * 128 : (i + 1) * 128].astype(F32).T.astype(BF16)
        for h in range(2):
            xt[h, i * 64 : (i + 1) * 64, :] = turned[h * 64 : (h + 1) * 64]

    xh2, x2 = turn(xh, 1, xh_n), turn(x, 1, x_n)

    def a2(k, back):
        dom_, x_ = dom_of(xh2 if k // 2 else xh, y, c), x2 if k % 2 else x
        ref = g_all.at[dom_ if back else dom, pl.ds((x_ if back else x) * z_n, z_n)]
        return pltpu.make_async_remote_copy(
            src_ref=ref,
            dst_ref=ref,
            send_sem=a2_s.at[k - 1],
            recv_sem=a2_r.at[k - 1],
            device_id=dev(dom_, x_=x_),
            device_id_type=MESH,
        )

    for d in range(1, z_n):
        a1(d, True).wait_recv()
    for k in range(1, 4):
        a2(k, False).start()
        pending.append(a2(k, False).wait_send)

    def y_ring(j, xh_):
        half = g_all.shape[1] // 2
        return Ring(
            lambda i: g_all.at[dom_of(xh_, i, c)],
            lambda i, h: g_all.at[dom_of(xh_, i, c), pl.ds(h * half, half)],
            y,
            y_n,
            lambda i: dev(dom_of(xh, i, c)),
            y_s.at[j],
            y_r.at[j],
        )

    def core(j, dy, back):
        ref = g_all.at[dom_of(xh2 if j else xh, turn(y, dy, y_n), turn(c, 1, c_n) if back else c)]
        return pltpu.make_async_remote_copy(
            src_ref=ref,
            dst_ref=ref,
            send_sem=core_s.at[j, dy],
            recv_sem=core_r.at[j, dy],
            device_id=dev(dom_of(xh, y, turn(c, 1, c_n))),
            device_id_type=MESH,
        )

    blk, col_blocks = w_ref.shape[0], x_ref.shape[1] // 128
    r_rows = blk // col_blocks
    per = 16 // r_rows
    rows = blk * per
    o = lax.broadcasted_iota(jnp.int32, (rows, rows), 0)
    j_ = lax.broadcasted_iota(jnp.int32, (rows, rows), 1)
    perm = (
        (j_ == (lax.rem(o, 16) // r_rows) * blk + (o // 16) * r_rows + lax.rem(o, r_rows)).astype(F32).astype(BF16)
    )

    def assemble(dom_):
        for t in range(g_all.shape[1] // per):
            blocks = [g_all[dom_, (b % x_n) * z_n + b // x_n] for b in range(t * per, (t + 1) * per)]
            part = jnp.dot(perm, jnp.concatenate(blocks, 0), preferred_element_type=F32).astype(BF16)
            row = pl.multiple_of((dom_ * (g_all.shape[1] // per) + t) * 16, 16)
            for cb in range(col_blocks):
                w_full[pl.ds(row, 16), cb * 128 : (cb + 1) * 128] = part[cb * 16 : (cb + 1) * 16]

    def rebuild(zb):
        groups = books.shape[1] // 64

        def per_group(gi, carry):
            r = pl.multiple_of(gi * 64, 64)
            table = books[zb, pl.ds(r, 64), :].astype(F32)
            out_row = pl.multiple_of(zb * books.shape[1] + r, 64)
            code_row = pl.multiple_of((zb * groups + gi) * 8, 8)

            def per_block(i, inner):
                for u in range(2):
                    p0 = pl.multiple_of(i * 256 + u * 128, 128)
                    cc = codes_t[pl.ds(code_row, 8), pl.ds(p0, 128)]
                    for jj in range(4):
                        parts = []
                        for j in (2 * jj, 2 * jj + 1):
                            idx = jnp.broadcast_to(cc[j : j + 1, :], (8, 128))
                            low = idx & 127
                            lo = jnp.take_along_axis(
                                table[j * 8 : j * 8 + 8, :128], low, axis=1, mode="promise_in_bounds"
                            )
                            hi = jnp.take_along_axis(
                                table[j * 8 : j * 8 + 8, 128:], low, axis=1, mode="promise_in_bounds"
                            )
                            parts.append(jnp.where(idx >= 128, hi, lo))
                        pt[pl.ds(pl.multiple_of(out_row + jj * 16, 16), 16), pl.ds(p0, 128)] = jnp.concatenate(
                            parts, 0
                        ).astype(BF16)
                return inner

            return lax.fori_loop(0, n_pass // 256, per_block, carry)

        lax.fori_loop(0, groups, per_group, 0)

    ring0, ring1 = y_ring(0, xh), y_ring(1, xh2)
    pending += [ring0.finish, ring1.finish]
    pending += [core(j, dy, False).wait_send for j in range(2) for dy in range(y_n)]
    a2(1, True).wait_recv()
    ring0.start(0)
    core(0, 0, False).start()
    a2(2, True).wait_recv()
    a2(3, True).wait_recv()
    ring1.start(0)
    core(1, 0, False).start()
    rebuild(z)
    book_ring.recv(0)
    book_ring.start(1)
    rebuild(turn(z, 1, z_n))
    ring0.recv(0)
    ring0.start(1)
    core(0, 1, False).start()
    core(0, 3, False).start()
    rebuild(turn(z, -1, z_n))
    book_ring.recv(1)
    book_ring.start(2)
    ring1.recv(0)
    ring1.start(1)
    core(1, 1, False).start()
    core(1, 3, False).start()
    assemble(dom_of(xh, y, c))
    assemble(dom_of(xh2, y, c))
    ring0.recv(1)
    core(0, 2, False).start()
    book_ring.recv(2)
    book_ring.start(3)
    for dy in (1, 3):
        assemble(dom_of(xh, turn(y, dy, y_n), c))
        assemble(dom_of(xh2, turn(y, dy, y_n), c))
    ring1.recv(1)
    core(1, 2, False).start()
    for j in range(2):
        assemble(dom_of(xh2 if j else xh, turn(y, 2, y_n), c))
    for dy in (0, 1, 3, 2):
        for j in range(2):
            core(j, dy, True).wait_recv()
            assemble(dom_of(xh2 if j else xh, turn(y, dy, y_n), turn(c, 1, c_n)))

    d_model = x_ref.shape[1]
    squares = jnp.zeros((1, 128), F32)
    for i in range(d_model // 256):
        enc = jnp.dot(x_ref[...], w_full[:, i * 256 : (i + 1) * 256], preferred_element_type=F32)
        for h in range(2):
            enc_t = enc[:, h * 128 : (h + 1) * 128].T
            squares = squares + jnp.sum(enc_t * enc_t, axis=0, keepdims=True)
            normed_t[i * 256 + h * 128 : i * 256 + (h + 1) * 128, :] = enc_t
    inv_rms = lax.rsqrt(squares / d_model + EPS)
    for i in range(d_model // 128):
        value = normed_t[i * 128 : (i + 1) * 128, :] * inv_rms
        normed_t[i * 128 : (i + 1) * 128, :] = value
        qs[z, i * 128 : (i + 1) * 128, :] = value.astype(BF16)

    half_d = d_model // 2
    right, left = dev(z_=turn(z, 1, z_n)), dev(z_=turn(z, -1, z_n))
    q_ring = HalfRing(lambda i, h: qs.at[i, pl.ds(h * half_d, half_d)], z, z_n, right, left, q_s, q_r)
    q_ring.start(0)
    q_ring.start(1)
    pending.append(q_ring.finish)
    rebuild(turn(z, 2, z_n))
    rebuild(turn(z, -2, z_n))
    q_ring.pass_on(0)
    rebuild(turn(z, 3, z_n))
    rebuild(turn(z, -3, z_n))
    q_ring.pass_on(1)
    book_ring.recv(3)
    rebuild(turn(z, 4, z_n))
    q_ring.pass_on(2)

    def flip(i, carry):
        f0 = pl.multiple_of(i * 128, 128)
        for t in range(n_pass // 128):
            pas[t * 128 : (t + 1) * 128, pl.ds(f0, 128)] = (
                pt[pl.ds(f0, 128), t * 128 : (t + 1) * 128].astype(F32).T.astype(BF16)
            )
        return carry

    lax.fori_loop(0, d_model // 128, flip, 0)

    sub8 = lax.broadcasted_iota(jnp.int32, (8, 128), 0)

    def score(j, totals):
        b = turn(z, j, z_n)
        block = qs[b]
        q_cat[:, j * 128 : (j + 1) * 128] = block
        total = jnp.zeros((1, 128), F32)
        for t in range(n_pass // 256):
            s = jnp.dot(pas[t * 256 : (t + 1) * 256, :], block, preferred_element_type=F32)
            e = jnp.exp(s)
            exps[j, t * 256 : (t + 1) * 256, :] = e
            total = total + jnp.sum(e, axis=0, keepdims=True)
        return totals + jnp.where(sub8 == b, jnp.broadcast_to(total, (8, 128)), 0.0)

    totals = score(0, jnp.zeros((8, 128), F32))
    q_ring.pass_on(3)
    totals = score(1, totals)
    totals = score(7, totals)
    q_ring.pass_on(4)
    totals = score(2, totals)
    totals = score(6, totals)
    q_ring.pass_on(5)
    totals = score(3, totals)
    totals = score(5, totals)
    q_ring.pass_on(6)
    totals = score(4, totals)

    tots[z] = totals

    def tot(d, back):
        other = turn(z, -d if back else d, z_n)
        ref = tots.at[other if back else z]
        return pltpu.make_async_remote_copy(
            src_ref=ref,
            dst_ref=ref,
            send_sem=tot_s.at[d - 1],
            recv_sem=tot_r.at[d - 1],
            device_id=dev(z_=other),
            device_id_type=MESH,
        )

    for d in range(1, z_n):
        tot(d, False).start()
        pending.append(tot(d, False).wait_send)
    for d in range(1, z_n):
        tot(d, True).wait_recv()
    totals = tots[0]
    for i in range(1, z_n):
        totals = totals + tots[i]
    inverse = 1.0 / totals

    sub16 = lax.broadcasted_iota(jnp.int32, (16, 128), 0)
    first = z * n_pass
    weights_all, pos_all = wt_ref[...], pos_ref[...]

    def grads(j):
        b = turn(z, j, z_n)
        inv = jnp.sum(jnp.where(sub8 == b, inverse, 0.0), axis=0, keepdims=True)
        wt = jnp.sum(jnp.where(sub16 == b * x_n + x, weights_all, 0.0), axis=0, keepdims=True)
        pos = jnp.sum(jnp.where(sub16 == b * x_n + x, pos_all, 0), axis=0, keepdims=True) - first
        for t in range(n_pass // 256):
            e = exps[j, t * 256 : (t + 1) * 256, :]
            ids = lax.broadcasted_iota(jnp.int32, (256, 128), 0) + t * 256
            prob = e * inv
            gs_cat[t * 256 : (t + 1) * 256, j * 128 : (j + 1) * 128] = (
                wt * jnp.where(ids == pos, prob - 1.0, prob)
            ).astype(BF16)
        block = gs_cat[:, j * 128 : (j + 1) * 128]
        for t in range(d_model // 256):
            gn[j, t * 256 : (t + 1) * 256, :] = jnp.dot(
                pt[t * 256 : (t + 1) * 256, :], block, preferred_element_type=F32
            )

    gn_ring = RingSum(
        lambda j, h: gn.at[j, pl.ds(h * half_d, half_d)], (gn_out, gn_out_step, gn_in, gn_in_step), z_n, right, left, gn_s, gn_r
    )
    pending.append(gn_ring.finish)
    grads(4)
    gn_ring.send(0)
    grads(3)
    grads(5)
    gn_ring.send(1)
    gn_ring.absorb(0)
    grads(2)
    grads(6)
    gn_ring.absorb(1)
    grads(1)
    grads(7)
    grads(0)

    def passage_grads(i, carry):
        p0 = pl.multiple_of(i * 256, 256)
        gpt[:, pl.ds(p0, 256)] = lax.dot_general(
            q_cat[...], gs_cat[pl.ds(p0, 256), :], NT, preferred_element_type=F32
        )
        return carry

    lax.fori_loop(0, n_pass // 256, passage_grads, 0)

    gn_ring.absorb(2)

    levels = lax.broadcasted_iota(jnp.int32, (64, n_pass), 0).astype(BF16)

    def scatter(lo_m, hi_m):
        def per_subs(i, carry):
            for u in range(4):
                m = i * 4 + u
                r = pl.multiple_of(m * 8, 8)
                code = codes_t[pl.ds(m, 1), :]
                low = (code & 63).astype(BF16)
                high = jnp.broadcast_to(lax.shift_right_logical(code, 6).astype(BF16), (16, n_pass))
                g = gpt[pl.ds(r, 8), :]
                g_hi = g.astype(BF16).astype(F32)
                g16 = jnp.concatenate([g_hi, g - g_hi], 0).astype(BF16)
                left = jnp.concatenate([jnp.where(high == BF16(h), g16, BF16(0)) for h in range(4)], 0)
                onehot = jnp.where(levels == jnp.broadcast_to(low, (64, n_pass)), BF16(1), BF16(0))
                out = lax.dot_general(left, onehot, NT, preferred_element_type=F32)
                cg[pl.ds(r, 8), :] = jnp.concatenate(
                    [out[h * 16 : h * 16 + 8] + out[h * 16 + 8 : h * 16 + 16] for h in range(4)], 1
                )
            return carry

        lax.fori_loop(lo_m // 4, hi_m // 4, per_subs, 0)

    own_rows = cg.shape[0] // (z_n * x_n)

    def own_words(zb, dp):
        return pl.ds(pl.multiple_of((zb * x_n + dp) * own_rows, own_rows), own_rows)

    def to_pair(zb):
        return pltpu.make_async_remote_copy(
            src_ref=cg.at[own_words(zb, turn(x, 1, x_n))],
            dst_ref=cg_x.at[zb],
            send_sem=cx_s.at[zb],
            recv_sem=cx_r.at[zb],
            device_id=dev(x_=turn(x, 1, x_n)),
            device_id_type=MESH,
        )

    def scatter_block(zb):
        scatter(zb * n_sub // z_n, (zb + 1) * n_sub // z_n)
        to_pair(zb).start()
        pending.append(to_pair(zb).wait_send)

    for zb in range(4):
        scatter_block(zb)
        gn_ring.absorb(zb + 3)

    inner = jnp.zeros((1, 128), F32)
    for i in range(d_model // 256):
        part = slice(i * 256, (i + 1) * 256)
        inner = inner + jnp.sum(gn[0, part, :] * normed_t[part, :], axis=0, keepdims=True)
    inner = inner / d_model
    for i in range(d_model // 256):
        part = slice(i * 256, (i + 1) * 256)
        ge_t[part, :] = (inv_rms * (gn[0, part, :] - normed_t[part, :] * inner)).astype(BF16)

    def share(i, core_, right_half):
        out = lax.dot_general(
            xt[core_], ge_t[half_d:, :] if right_half else ge_t[:half_d, :], NT, preferred_element_type=F32
        )
        for xh_ in range(xh_n):
            for y_ in range(y_n):
                for z_ in range(z_n):
                    tile = out[((xh_ * y_n + y_) * z_n + z_) * 8 : ((xh_ * y_n + y_) * z_n + z_) * 8 + 8]
                    if right_half:
                        wz[i, z_, xh_, y_] = tile
                    else:
                        wy[i, y_, xh_, z_] = tile

    sibling = turn(c, 1, c_n)

    def to_core(i):
        buf = (wz, wy)[i]
        return pltpu.make_async_remote_copy(
            src_ref=buf.at[1],
            dst_ref=buf.at[2],
            send_sem=wc_s.at[i],
            recv_sem=wc_r.at[i],
            device_id=dev(dom_of(xh, y, sibling)),
            device_id_type=MESH,
        )

    share(1, sibling, True)
    to_core(0).start()
    share(1, sibling, False)
    to_core(1).start()
    share(0, c, True)
    share(0, c, False)
    pending += [to_core(0).wait_send, to_core(1).wait_send]

    wz_ring = RingSum(
        lambda j, h: wz.at[0, turn(z, j, z_n), h], (wz_out, wz_out_step, wz_got, wz_got_step), z_n, right, left, wz_s, wz_r
    )
    wy_ring = RingSum(
        lambda j, h: wy.at[0, turn(y, j, y_n), h],
        (wy_out, wy_out_step, wy_got, wy_got_step),
        y_n,
        dev(dom_of(xh, turn(y, 1, y_n), c)),
        dev(dom_of(xh, turn(y, -1, y_n), c)),
        wy_s,
        wy_r,
    )

    def cg_half(j, h):
        row = (turn(z, j, z_n) * x_n + x) * own_rows + h * (own_rows // 2)
        return cg.at[pl.ds(pl.multiple_of(row, own_rows // 2), own_rows // 2)]

    cg_ring = RingSum(cg_half, (cg_out, cg_out_step, cg_in, cg_in_step), z_n, right, left, cz_s, cz_r)
    pending += [wz_ring.finish, wy_ring.finish, cg_ring.finish]

    to_core(0).wait_recv()
    for i in range(z_n):
        wz[0, i] += wz[2, i]
    for i in range(2):
        wz_ring.send(i)
    to_core(1).wait_recv()
    for i in range(y_n):
        wy[0, i] += wy[2, i]
    for i in range(2):
        wy_ring.send(i)
    def direct(bufs, send_sem, recv_sem, d, target):
        out, out_step, got, got_step = bufs
        return [
            pltpu.make_async_remote_copy(
                src_ref=src.at[d - 1],
                dst_ref=dst.at[d - 1],
                send_sem=send_sem.at[d - 1, t],
                recv_sem=recv_sem.at[d - 1, t],
                device_id=target,
                device_id_type=MESH,
            )
            for t, (src, dst) in enumerate(((out, got), (out_step, got_step)))
        ]

    wzy_bufs = (wzy_out, wzy_out_step, wzy_in, wzy_in_step)
    wyz_bufs = (wyz_out, wyz_out_step, wyz_in, wyz_in_step)

    def wzy(d):
        return direct(wzy_bufs, wzy_s, wzy_r, d, dev(dom_of(xh, turn(y, d, y_n), c)))

    def wyz(d):
        return direct(wyz_bufs, wyz_s, wyz_r, d, dev(z_=turn(z, d, z_n)))

    def spread(view, bufs, copies, n):
        for d in range(1, n):
            bufs[0][d - 1], bufs[1][d - 1] = quantize(view(d).reshape(xh_n * 8, half_d))
            for copy in copies(d):
                copy.start()
                pending.append(copy.wait_send)

    def collect(view, bufs, copies, n):
        acc = view(0).reshape(xh_n * 8, half_d)
        for d in range(1, n):
            for copy in copies(d):
                copy.wait_recv()
            acc = acc + restore(bufs[2][d - 1], bufs[3][d - 1])
        return acc.reshape(xh_n, 8, half_d)

    def wz_part(d):
        return wz[0, z, :, turn(y, d, y_n)]

    def wy_part(d):
        return wy[0, y, :, turn(z, d, z_n)]

    for i in range(3):
        scatter_block(4 + i)
        wz_ring.absorb(i)
        wy_ring.absorb(i)
    spread(wy_part, wyz_bufs, wyz, z_n)
    scatter_block(7)
    wz_ring.absorb(3)
    for zb in range(z_n):
        to_pair(zb).wait_recv()
        cg[own_words(zb, x), :] += cg_x[zb]
    for i in range(2):
        cg_ring.send(i)
    for i in range(3):
        wz_ring.absorb(4 + i)
        cg_ring.absorb(i)
    spread(wz_part, wzy_bufs, wzy, y_n)
    cg_ring.absorb(3)
    def last(k, h):
        xh_, x_ = turn(xh, k // 2, xh_n), turn(x, k % 2, x_n)
        columns = pl.ds(h * half_d, half_d)
        return pltpu.make_async_remote_copy(
            src_ref=total.at[xh_, :, columns],
            dst_ref=final.at[k - 1, :, columns],
            send_sem=fin_s.at[k - 1, h],
            recv_sem=fin_r.at[k - 1, h],
            device_id=dev(dom_of(xh_, y, c), x_=x_),
            device_id_type=MESH,
        )

    for h, args in ((0, (wy_part, wyz_bufs, wyz, z_n)), (1, (wz_part, wzy_bufs, wzy, y_n))):
        total[:, :, h * half_d : (h + 1) * half_d] = collect(*args)
        for k in range(1, 4):
            last(k, h).start()
            pending.append(last(k, h).wait_send)
    for i in range(4, 7):
        cg_ring.absorb(i)
    cg_ref[...] = cg[own_words(z, x), :]
    acc = total[xh]
    for k in range(1, 4):
        for h in range(2):
            last(k, h).wait_recv()
        acc = acc + final[k - 1]
    wg_ref[...] = jnp.where(x == 0, acc[:4], acc[4:])

    for wait in pending:
        wait()


def per_device(sizes, queries_in, encoder_weight, codebook, codes, positive_ids, loss_weight):
    xh_n, y_n, c_n, z_n, x_n = sizes
    q_rows, d_model = queries_in.shape[1:]
    w_rows = encoder_weight.shape[0]
    subs, width, words = codebook.shape[1:]
    n_pass, n_sub = codes.shape[1:]
    blk = w_rows * d_model // 128
    group, doms, half = z_n * x_n, xh_n * y_n * c_n, d_model // 2
    w = encoder_weight.reshape(w_rows, d_model // 128, 128).transpose(1, 0, 2).reshape(blk, 128)

    def ring_bufs(n, rows, lanes):
        return 2 * [
            pltpu.VMEM((2, n - 1, rows, lanes), jnp.int16),
            pltpu.VMEM((2, n - 1, 8 if rows == 512 else 1, lanes), F32),
        ]

    def direct_bufs(n, rows, lanes):
        return 2 * [pltpu.VMEM((n - 1, rows, lanes), jnp.int16), pltpu.VMEM((n - 1, 1, lanes), F32)]

    vmem = pl.BlockSpec(memory_space=pltpu.VMEM)
    dma = pltpu.SemaphoreType.DMA
    wg, cg = pl.pallas_call(
        functools.partial(kernel, sizes),
        out_shape=(
            jax.ShapeDtypeStruct((w_rows, d_model), F32),
            jax.ShapeDtypeStruct((d_model // group, words), F32),
        ),
        in_specs=[vmem] * 6,
        out_specs=(vmem, vmem),
        scratch_shapes=[
            pltpu.VMEM((doms, group, blk, 128), BF16),
            pltpu.VMEM((d_model, d_model), BF16),
            pltpu.VMEM((2, d_model // 2, q_rows), BF16),
            pltpu.VMEM((z_n, subs * width, words), BF16),
            pltpu.VMEM((n_sub, n_pass), jnp.int32),
            pltpu.VMEM((d_model, n_pass), BF16),
            pltpu.VMEM((n_pass, d_model), BF16),
            pltpu.VMEM((z_n, d_model, q_rows), BF16),
            pltpu.VMEM((d_model, z_n * q_rows), BF16),
            pltpu.VMEM((z_n, n_pass, q_rows), F32),
            pltpu.VMEM((n_pass, z_n * q_rows), BF16),
            pltpu.VMEM((z_n, d_model, q_rows), F32),
            pltpu.VMEM((d_model, n_pass), F32),
            pltpu.VMEM((d_model, q_rows), F32),
            pltpu.VMEM((z_n, 8, 128), F32),
            pltpu.VMEM((d_model, q_rows), BF16),
            pltpu.VMEM((d_model, words), F32),
            pltpu.VMEM((z_n, d_model // group, words), F32),
            pltpu.VMEM((3, z_n, xh_n, y_n, 8, half), F32),
            pltpu.VMEM((3, y_n, xh_n, z_n, 8, half), F32),
            *direct_bufs(y_n, xh_n * 8, half),
            *direct_bufs(z_n, xh_n * 8, half),
            pltpu.VMEM((xh_n, 8, d_model), F32),
            pltpu.VMEM((3, 8, d_model), F32),
            *ring_bufs(z_n, half, q_rows),
            *ring_bufs(z_n, d_model // group // 2, words),
            *ring_bufs(z_n, y_n * 8, half),
            *ring_bufs(y_n, z_n * 8, half),
            dma((z_n - 1,)),
            dma((z_n - 1,)),
            dma((3,)),
            dma((3,)),
            dma((2, 2, y_n // 2)),
            dma((2, 2, y_n // 2)),
            dma((2, y_n)),
            dma((2, y_n)),
            dma((2, z_n // 2)),
            dma((2, z_n // 2)),
            dma((2, z_n - 1)),
            dma((2, z_n - 1)),
            dma((z_n - 1,)),
            dma((z_n - 1,)),
            dma((2, z_n - 1, 2)),
            dma((2, z_n - 1, 2)),
            dma((z_n,)),
            dma((z_n,)),
            dma((2, z_n - 1, 2)),
            dma((2, z_n - 1, 2)),
            dma((2,)),
            dma((2,)),
            dma((2, z_n - 1, 2)),
            dma((2, z_n - 1, 2)),
            dma((2, y_n - 1, 2)),
            dma((2, y_n - 1, 2)),
            dma((y_n - 1, 2)),
            dma((y_n - 1, 2)),
            dma((z_n - 1, 2)),
            dma((z_n - 1, 2)),
            dma((3, 2)),
            dma((3, 2)),
        ],
        compiler_params=pltpu.CompilerParams(
            collective_id=0, has_side_effects=True, vmem_limit_bytes=60 * 2**20
        ),
        name="encoder_codebook_grads",
    )(
        w,
        queries_in[0],
        codebook.reshape(subs * width, words),
        codes[0],
        positive_ids.reshape(group, q_rows),
        loss_weight.reshape(group, q_rows).astype(F32),
    )
    return wg, cg.reshape(1, n_sub // group, width, words)


def solution(mesh):
    doms = mesh.shape["dom"]
    sizes = (2, doms // 4, 2, mesh.shape["shard"], mesh.shape["dp"])
    return jax.shard_map(
        functools.partial(per_device, sizes),
        mesh=mesh,
        in_specs=(
            P("dom", ("shard", "dp"), None),
            P(("dom", "shard", "dp"), None),
            P("dom", "shard", None, None),
            P("dom", "shard", None),
            P("dom", None),
            P("dom", None),
        ),
        out_specs=(P(("dom", "shard", "dp"), None), P("dom", ("shard", "dp"), None, None)),
        check_vma=False,
    )
```
